32 devices in a mesh: band: 2 (over core), dom: 16 (over z, y, x).
Axes of the slice: x: 2, y: 2, z: 4, core: 2. Of those that a mesh axis runs over, the one named last changes fastest.
Arguments:
- orbital_block: bfloat16 [4096, 1024], P('dom', 'band'), may hold values from -6 to 6
- cell_matrices: bfloat16 [64, 125, 125], P('dom'), may hold values from -0.09 to 0.09, as said below
- cell_nodes: int32 [125, 64], P(None, 'dom'), may hold values from 0 to 319, as said below
- shared_nodes: int32 [16, 64], P('dom'), may hold values from 0 to 255, as said below
- inv_sqrt_mass: float32 [4096], P('dom'), may hold values from 0.8 to 1.25
- potential: float32 [4096], P('dom'), may hold values from -0.5 to 0.3
- filter_center: float32 [1], replicated, may hold values from -0.1 to 0.1
- filter_halfwidth: float32 [1], replicated, may hold values from 0.8 to 1.2
Outputs:
- filtered: bfloat16 [4096, 1024], P('dom', 'band')
- intersection: float32 [1024, 1024], P(('band', 'dom'))
- projected: float32 [1024, 1024], P(('band', 'dom'))
The draws below stay inside these ranges and needn't reach their ends.
Inputs may be any that keep to these rules, and one draw needn't show every extreme that they name: `cell_matrices`: each cell's matrix is symmetric. `cell_nodes`: column c lists the 125 nodes of cell c, a hexahedron of degree 4 with its nodes in lexicographic order, numbered as the device that holds the cell sees them: a value below 256 is one of its own nodes, a value 256 + j is entry j of the next device's (cyclically) shared list. Every own node and every shared entry is used by some cell. `shared_nodes`: row d holds 64 distinct own nodes of device d, which cells of device d - 1 (cyclically) also use.
All inputs are finite; a program needn't handle non-finite values.
Results may differ from the reference program's by a relative error of at most 0.024.
Values may be sent and summed in bfloat16 or wider, within the bound.
No kernel may reach another device: no remote copies, remote signals or barrier semaphores. Data moves between devices by JAX's collectives and lax.ppermute only.
A program may use at most 64 MiB of HBM per device.

```python
import math
import jax
import jax.numpy as jnp
from jax import lax

ORB_BLK = 512
FILTER_DEG = 4
CY = 2
CZ = 2
CELLS_DEV = 4
PLANE = 64
NODES_DEV = 256
NODES_ALL = 4096
CELLS_ALL = 64
ORB = 1024
N_BAND = 2
N_DOM = 16


def mesh_tables(key):
    span_y = 4 * CY
    span_z = 4 * CZ
    perm_keys = jax.random.split(jax.random.fold_in(key, 4242), N_DOM)
    orders = jax.vmap(lambda one_key: jax.random.permutation(one_key, NODES_DEV))(perm_keys).astype(jnp.int32)
    corner = jnp.arange(125, dtype=jnp.int32)
    along_x = corner // 25
    along_y = corner // 5 % 5
    along_z = corner % 5
    cells = jnp.arange(CELLS_DEV, dtype=jnp.int32)
    cell_y = cells // CZ
    cell_z = cells % CZ
    ypos = (4 * cell_y[None, :] + along_y[:, None]) % span_y
    zpos = (4 * cell_z[None, :] + along_z[:, None]) % span_z
    xpos = jnp.broadcast_to(along_x[:, None], ypos.shape)
    inplane = ypos * span_z + zpos
    canon = jnp.minimum(xpos, 3) * span_y * span_z + inplane

    def per_device(order):
        return jnp.where(xpos < 4, order[canon], NODES_DEV + inplane).astype(jnp.int32)
    tables = jax.vmap(per_device)(orders)
    cell_table = jnp.transpose(tables, (1, 0, 2)).reshape(125, N_DOM * CELLS_DEV)
    shared = orders[:, :PLANE]
    return (cell_table.astype(jnp.int32), shared.astype(jnp.int32))


def draw_cell_nodes(key, part):
    return mesh_tables(key)[0]


def draw_shared_nodes(key, part):
    return mesh_tables(key)[1]


def draw_cell_matrices(key, part):
    spread = 4000.0 ** (-0.5)
    inner = jax.random.fold_in(key, 777)
    raw = jax.random.normal(inner, (CELLS_ALL, 125, 125), jnp.float32) * spread
    sym = (raw + jnp.transpose(raw, (0, 2, 1))) * 0.70710678
    return jnp.clip(sym, -0.09, 0.09).astype(jnp.bfloat16)


def block_levels(rng, extent, cuts, smallest, high):
    def one(position, shards_of):
        steps = jax.random.uniform(jax.random.fold_in(jax.random.fold_in(rng, 6), position), (shards_of,), jnp.float32, smallest / len(cuts), high / len(cuts))
        return jnp.repeat(jnp.exp(steps), extent[position] // shards_of).reshape((-1,) + (1,) * (len(extent) - position - 1))

    loudness = one(*cuts[0])
    for cut in cuts[1:]:
        loudness = loudness * one(*cut)
    return loudness


def noise(key, dims, deviation, most, shards=(), kind=jnp.bfloat16):
    array = jax.random.normal(key, dims, jnp.float32) * deviation
    if len(shards) > 0:
        array = block_levels(key, dims, shards, -0.22, 0.18) * array
    return jnp.clip(array, min=-most, max=most).astype(kind)


def setup_inputs(seed: int = 0) -> dict:
    streams_of = jax.random.split(jax.random.key(seed), 9)
    return {
        "orbital_block": noise(streams_of[0], (NODES_ALL, ORB), 1.0, 6.0, ((0, 16), (1, 2))),
        "cell_matrices": draw_cell_matrices(jax.random.fold_in(streams_of[8], 71), 0),
        "cell_nodes": draw_cell_nodes(jax.random.fold_in(streams_of[8], 71), 0),
        "shared_nodes": draw_shared_nodes(jax.random.fold_in(streams_of[8], 71), 0),
        "inv_sqrt_mass": jnp.clip(jnp.exp(math.log(1.25) - 0.4462871 * jax.random.uniform(streams_of[4], (NODES_ALL,), jnp.float32) ** block_levels(streams_of[4], (NODES_ALL,), ((0, 16),), -0.2, 0.2)), 0.8, 1.25),
        "potential": jnp.clip(-0.5 + 0.8 * jax.random.uniform(streams_of[5], (NODES_ALL,), jnp.float32) ** block_levels(streams_of[5], (NODES_ALL,), ((0, 16),), -0.2, 0.2), -0.5, 0.3),
        "filter_center": jnp.clip(jax.random.uniform(streams_of[6], (1,), jnp.float32, -0.1, 0.1), -0.1, 0.1),
        "filter_halfwidth": jnp.clip(jax.random.uniform(streams_of[7], (1,), jnp.float32, 0.8, 1.2), 0.8, 1.2),
    }


def hamilton(field, global_nodes, cell_matrices, inv_sqrt_mass, potential):
    scaled = (inv_sqrt_mass[:, None] * field).astype(jnp.bfloat16)
    gathered = scaled[global_nodes].astype(jnp.float32)
    cell_out = jnp.einsum('cij,jck->ick', cell_matrices.astype(jnp.float32), gathered)
    columns = field.shape[1]
    assembled = jnp.zeros(field.shape, jnp.float32).at[global_nodes.reshape(-1)].add(cell_out.reshape(-1, columns))
    return inv_sqrt_mass[:, None] * assembled + potential[:, None] * field

def reference(orbital_block, cell_matrices, cell_nodes, shared_nodes, inv_sqrt_mass, potential, filter_center, filter_halfwidth):
    cell_dev = jnp.arange(CELLS_ALL, dtype=jnp.int32) // CELLS_DEV
    next_dev = (cell_dev + 1) % N_DOM
    ghost_slot = jnp.clip(cell_nodes - NODES_DEV, 0, PLANE - 1).astype(jnp.int32)
    remote = next_dev[None, :] * NODES_DEV + shared_nodes[next_dev[None, :], ghost_slot]
    global_nodes = jnp.where(cell_nodes < NODES_DEV, cell_dev[None, :] * NODES_DEV + cell_nodes, remote).astype(jnp.int32)

    def mapped(field):
        applied_field = hamilton(field, global_nodes, cell_matrices, inv_sqrt_mass, potential)
        return (applied_field - filter_center[0] * field) / filter_halfwidth[0]

    def filter_one(columns):
        previous = columns.astype(jnp.float32)
        current = mapped(previous)
        for degree_step in range(FILTER_DEG - 1):
            following = 2.0 * mapped(current) - previous
            previous = current
            current = following
        filtered_part = current.astype(jnp.bfloat16)
        applied_part = hamilton(filtered_part.astype(jnp.float32), global_nodes, cell_matrices, inv_sqrt_mass, potential).astype(jnp.bfloat16)
        return (filtered_part, applied_part)
    pieces = orbital_block.reshape(NODES_ALL, N_BAND, ORB_BLK).transpose(1, 0, 2)
    filtered_blocks, applied_blocks = lax.map(filter_one, pieces)
    filtered = filtered_blocks.transpose(1, 0, 2).reshape(NODES_ALL, ORB)
    applied = applied_blocks.transpose(1, 0, 2).reshape(NODES_ALL, ORB)
    factor = 1.0 / NODES_ALL
    intersection = jnp.dot(filtered.T, filtered, preferred_element_type=jnp.float32) * factor
    projected = jnp.dot(filtered.T, applied, preferred_element_type=jnp.float32) * factor
    return (filtered, intersection, projected)
```

```python
import functools

import jax
import jax.numpy as jnp
from jax import lax
from jax.experimental import pallas as pl
from jax.experimental.pallas import tpu as pltpu
from jax.sharding import PartitionSpec as P

FILTER_DEG = 4
GROUP = 4
LANES = 128
EXTRA = 32
F32 = jnp.float32
BF16 = jnp.bfloat16
VMEM_LIMIT = 48 * 1024 * 1024


def dot(a, b):
    return jnp.dot(a, b, preferred_element_type=F32)


def dot_nt(a, b):
    return lax.dot_general(a, b, (((1,), (1,)), ((), ())), preferred_element_type=F32)


def iota(shape, dim):
    return lax.broadcasted_iota(jnp.int32, shape, dim)


def split3(x):
    high = x.astype(BF16)
    rest = x - high.astype(F32)
    middle = rest.astype(BF16)
    low = (rest - middle.astype(F32)).astype(BF16)
    return high, middle, low


def pack_kernel(planes, place_ref, field_ref, cells_ref, nodes_ref, shared_ref, mass_ref, pot_ref, *outs):
    out_refs, turned = outs[:GROUP], outs[GROUP]
    place = place_ref[0]
    nodes, width = field_ref.shape
    cells, corners, _ = cells_ref.shape
    rows = LANES // planes
    source = iota((width, LANES), 0)
    target = iota((width, LANES), 1)
    turned[...] = jnp.zeros_like(turned)
    turned[0:corners, 0:cells] = nodes_ref[...].astype(F32)
    tables = jnp.transpose(turned[...])[0:8]
    lane = iota((8, LANES), 1)
    high = jnp.floor(tables * (1.0 / 64.0))
    low = tables - 64.0 * high
    high = jnp.where(lane < corners, high, -8.0)
    shared = jnp.concatenate(
        [shared_ref[...].astype(F32), jnp.zeros((1, LANES - shared_ref.shape[1]), F32)], axis=1
    )
    pieces = [high[0:cells], low[0:cells], shared]
    for value_ref in (mass_ref, pot_ref):
        pieces += [part.astype(F32) for part in split3(value_ref[...])]
    used = sum(piece.shape[0] for piece in pieces)
    pieces.append(jnp.zeros((EXTRA - used, LANES), F32))
    extra = jnp.concatenate(pieces, axis=0).astype(BF16)
    for k in range(GROUP):
        chunk = place ^ k
        pick = (target // rows) * (GROUP * rows) + chunk * rows + target % rows == source
        out_refs[k][0:nodes, :] = dot(field_ref[...], pick.astype(F32).astype(BF16)).astype(BF16)
        base = nodes
        for c in range(cells):
            out_refs[k][base + c * LANES : base + (c + 1) * LANES, :] = jnp.zeros((LANES, LANES), BF16)
            out_refs[k][base + c * LANES : base + c * LANES + corners, 0:corners] = cells_ref[c]
        out_refs[k][base + cells * LANES :, :] = extra


def apply_plane(own, down, up, fields, outside_u, outside_g, keep=None):
    shared = down[0].shape[0] // 2
    traces = [dot(down[i], fields[i]) for i in range(GROUP)]
    to_next = traces[GROUP - 1][:shared]
    to_previous = traces[0][shared:]
    w, g = outside_u, outside_g
    if callable(outside_u):
        w, g = outside_u(to_previous, to_next)
    sums = []
    for i in range(GROUP):
        if keep is not None and i not in keep:
            sums.append(None)
            continue
        below = w if i == 0 else traces[i - 1][:shared]
        above = g if i == GROUP - 1 else traces[i + 1][shared:]
        total = dot(own[i], fields[i])
        if below is None:
            below = jnp.zeros_like(to_next)
        if above is None:
            above = jnp.zeros_like(to_next)
        sides = jnp.concatenate([above, below], axis=0).astype(BF16)
        sums.append(total + dot(up[i], sides))
    return sums, traces


def first_kernel(
    cells, shared, place_ref, center_ref, half_ref, m0, m1, m2, m3,
    own_ref, down_ref, up_ref, mass_ref, scale_ref, diag_ref, start_ref, next_ref, previous_ref,
    raw, corner, cur, prev,
):
    place = place_ref[0]
    center, half = center_ref[0], half_ref[0]
    nodes = raw.shape[1]
    both = nodes + shared
    halves = nodes // LANES
    for k, ref in enumerate((m0, m1, m2, m3)):
        slab = place ^ k
        base = nodes + cells * LANES
        extra = ref[base : base + EXTRA, :].astype(F32)
        ids = (64.0 * extra[0:cells] + extra[cells : 2 * cells]).astype(jnp.int32)
        total = jnp.zeros((both, both), F32)
        for c in range(cells):
            pick = (iota((both, LANES), 0) == ids[c : c + 1]).astype(F32).astype(BF16)
            matrix = ref[nodes + c * LANES : nodes + (c + 1) * LANES, :]
            half_way = dot(pick, matrix).astype(BF16)
            total = total + dot_nt(half_way, pick)
        raw[slab] = total[:nodes, :nodes]
        corner[slab] = total[nodes:, nodes:]
        own_shared = extra[2 * cells : 2 * cells + 1, 0:shared].astype(jnp.int32)
        place_in = (iota((nodes, shared), 0) == own_shared).astype(F32)
        sides = jnp.concatenate([total[:nodes, nodes:], place_in], axis=1)
        up_ref[slab] = sides.astype(BF16)
        down_ref[slab] = jnp.transpose(sides).astype(BF16)
        row = 2 * cells + 1
        for h in range(halves):
            at = pl.ds(pl.multiple_of(slab * nodes + h * LANES, LANES), LANES)
            mass_row = sum(extra[row + j * halves + h : row + j * halves + h + 1] for j in range(3))
            off = row + 3 * halves
            pot_row = sum(extra[off + j * halves + h : off + j * halves + h + 1] for j in range(3))
            mass = jnp.transpose(jnp.broadcast_to(mass_row, (LANES, LANES)))
            pot = jnp.transpose(jnp.broadcast_to(pot_row, (LANES, LANES)))
            mass_ref[at, :] = mass
            scale_ref[at, :] = mass / half
            diag_ref[at, :] = (pot - center) / half
        start_ref[pl.ds(pl.multiple_of(slab * nodes, nodes), nodes), :] = ref[0:nodes, :]
    own_ref[0] = raw[0].astype(BF16)
    for i in range(1, GROUP):
        place_in = up_ref[i][:, shared:]
        moved = dot(place_in, corner[i - 1].astype(BF16)).astype(BF16)
        own_ref[i] = (raw[i] + dot_nt(moved, place_in)).astype(BF16)

    cur[:, 0:LANES] = start_ref[...].astype(F32)
    cur[:, LANES:] = jnp.zeros((GROUP * nodes, 2 * shared), F32)
    top = (GROUP - 1) * nodes
    first = up_ref[0].astype(F32)
    last = up_ref[GROUP - 1].astype(F32)
    lane = iota((nodes, 2 * shared), 1)
    swapped = jnp.concatenate([first[:, shared:], first[:, :shared]], axis=1)
    cur[0:nodes, LANES:] = jnp.where(lane < shared, swapped * scale_ref[0:nodes, :], 0.0)
    swapped = jnp.concatenate([last[:, shared:], last[:, :shared]], axis=1)
    cur[top:, LANES:] = cur[top:, LANES:] + jnp.where(lane >= shared, swapped * scale_ref[top:, :], 0.0)
    prev[...] = jnp.zeros_like(prev)

    own = [own_ref[i] for i in range(GROUP)]
    down = [down_ref[i] for i in range(GROUP)]
    up = [up_ref[i] for i in range(GROUP)]

    def wide(ref, i):
        part = ref[i * nodes : (i + 1) * nodes, :]
        return jnp.concatenate([part, part], axis=1)

    next_parts, previous_parts = [], []
    for k in range(FILTER_DEG):
        last_step = k == FILTER_DEG - 1
        if last_step:
            field0 = (mass_ref[0:nodes, :] * cur[0:nodes, 0:LANES]).astype(BF16)
            field3 = (mass_ref[top:, :] * cur[top:, 0:LANES]).astype(BF16)
            next_ref[k * shared : (k + 1) * shared, :] = dot(down[GROUP - 1], field3)[:shared].astype(BF16)
            previous_ref[k * shared : (k + 1) * shared, :] = dot(down[0], field0)[shared:].astype(BF16)
            break
        fields = [(wide(mass_ref, i) * cur[i * nodes : (i + 1) * nodes, :]).astype(BF16) for i in range(GROUP)]
        keep = None if k < FILTER_DEG - 2 else (0, GROUP - 1)
        sums, traces = apply_plane(own, down, up, fields, None, None, keep)
        to_next = traces[GROUP - 1][:shared]
        to_previous = traces[0][shared:]
        next_ref[k * shared : (k + 1) * shared, :] = to_next[:, 0:LANES].astype(BF16)
        previous_ref[k * shared : (k + 1) * shared, :] = to_previous[:, 0:LANES].astype(BF16)
        next_parts.append(to_next[:, LANES + shared :])
        previous_parts.append(to_previous[:, LANES : LANES + shared])
        for i in range(GROUP):
            if sums[i] is None:
                continue
            at = slice(i * nodes, (i + 1) * nodes)
            now = cur[at, :]
            image = wide(scale_ref, i) * sums[i] + wide(diag_ref, i) * now
            if k == 0:
                factor = jnp.where(iota((1, 2 * LANES), 1) < LANES, 1.0, 2.0)
                new = factor * image
            else:
                new = 2.0 * image - prev[at, :]
            prev[at, :] = now
            cur[at, :] = new
    at = FILTER_DEG * shared
    next_parts.append(corner[GROUP - 1])
    previous_parts.append(jnp.zeros((shared, shared), F32))
    for j in range(2):
        next_ref[at + j * shared : at + (j + 1) * shared, :] = jnp.concatenate(
            next_parts[2 * j : 2 * j + 2], axis=1
        ).astype(BF16)
        previous_ref[at + j * shared : at + (j + 1) * shared, :] = jnp.concatenate(
            previous_parts[2 * j : 2 * j + 2], axis=1
        ).astype(BF16)


def second_kernel(
    shared, own_ref, down_ref, up_ref, mass_ref, scale_ref, diag_ref, start_ref, sent_ref, below_ref, above_ref,
    filtered_ref, next_ref, previous_ref, cur, prev,
):
    nodes = own_ref.shape[1]
    own = [own_ref[i] for i in range(GROUP)]
    down = [down_ref[i] for i in range(GROUP)]
    up = [up_ref[i] for i in range(GROUP)]
    at = FILTER_DEG * shared
    near_b, far_b = below_ref[at : at + shared, :], below_ref[at + shared : at + 2 * shared, :]
    near_a, far_a = above_ref[at : at + shared, :], above_ref[at + shared : at + 2 * shared, :]
    mine = sent_ref[at + shared : at + 2 * shared, :]
    zero = jnp.zeros((shared, LANES), BF16)
    cur[...] = start_ref[...].astype(F32)
    prev[...] = jnp.zeros_like(prev)
    below_past, above_past = [], []

    def past(items, lag):
        if lag > len(items):
            return zero
        item = items[len(items) - lag]
        return item if lag == len(items) else item * 2

    def pair(a, b):
        return jnp.concatenate([a, b], axis=0)

    for k in range(FILTER_DEG):

        def outside(to_previous, to_next, k=k):
            here = to_previous.astype(BF16)
            below = below_ref[k * shared : (k + 1) * shared, :].astype(F32)
            below = below + dot(near_b, pair(past(below_past, 1), past(below_past, 2)))
            below = below + dot(far_b, pair(past(below_past, 3), here))
            above = above_ref[k * shared : (k + 1) * shared, :].astype(F32)
            above = above + dot(near_a, pair(past(above_past, 1), past(above_past, 2)))
            above = above + dot(far_a, pair(past(above_past, 3), zero))
            force = to_next + dot(mine, pair(zero, above.astype(BF16)))
            below_past.append(here)
            above_past.append(force.astype(BF16))
            return below, above

        fields = [
            (mass_ref[i * nodes : (i + 1) * nodes, :] * cur[i * nodes : (i + 1) * nodes, :]).astype(BF16)
            for i in range(GROUP)
        ]
        sums, _ = apply_plane(own, down, up, fields, outside, None)
        for i in range(GROUP):
            rows = slice(i * nodes, (i + 1) * nodes)
            now = cur[rows, :]
            image = scale_ref[rows, :] * sums[i] + diag_ref[rows, :] * now
            new = image if k == 0 else 2.0 * image - prev[rows, :]
            prev[rows, :] = now
            cur[rows, :] = new
    filtered_ref[...] = cur[...].astype(BF16)
    top = (GROUP - 1) * nodes
    field0 = (mass_ref[0:nodes, :] * filtered_ref[0:nodes, :].astype(F32)).astype(BF16)
    field3 = (mass_ref[top:, :] * filtered_ref[top:, :].astype(F32)).astype(BF16)
    next_ref[...] = dot(down[GROUP - 1], field3)[:shared].astype(BF16)
    previous_ref[...] = dot(down[0], field0)[shared:].astype(BF16)


def third_kernel(
    shared, center_ref, half_ref, own_ref, down_ref, up_ref, mass_ref, diag_ref, filtered_ref, corner_ref, below_ref,
    above_ref, applied_ref,
):
    nodes = own_ref.shape[1]
    center, half = center_ref[0], half_ref[0]
    own = [own_ref[i] for i in range(GROUP)]
    down = [down_ref[i] for i in range(GROUP)]
    up = [up_ref[i] for i in range(GROUP)]
    at = FILTER_DEG * shared
    far_b = corner_ref[at + shared : at + 2 * shared, :]
    zero = jnp.zeros((shared, LANES), BF16)

    def outside(to_previous, to_next):
        below = below_ref[...].astype(F32)
        below = below + dot(far_b, jnp.concatenate([zero, to_previous.astype(BF16)], axis=0))
        return below, above_ref[...].astype(F32)

    values = [filtered_ref[i * nodes : (i + 1) * nodes, :].astype(F32) for i in range(GROUP)]
    fields = [(mass_ref[i * nodes : (i + 1) * nodes, :] * values[i]).astype(BF16) for i in range(GROUP)]
    sums, _ = apply_plane(own, down, up, fields, outside, None)
    for i in range(GROUP):
        rows = slice(i * nodes, (i + 1) * nodes)
        pot = diag_ref[rows, :] * half + center
        applied_ref[rows, :] = (mass_ref[rows, :] * sums[i] + pot * values[i]).astype(BF16)


def call(kernel, outs, args, scalars=0, scratch=(), flops=0):
    in_specs = [pl.BlockSpec(memory_space=pltpu.SMEM)] * scalars
    in_specs += [pl.BlockSpec(memory_space=pltpu.VMEM)] * (len(args) - scalars)
    return pl.pallas_call(
        kernel,
        out_shape=[jax.ShapeDtypeStruct(shape, dtype) for shape, dtype in outs],
        in_specs=in_specs,
        out_specs=[pl.BlockSpec(memory_space=pltpu.VMEM)] * len(outs),
        scratch_shapes=list(scratch),
        compiler_params=pltpu.CompilerParams(vmem_limit_bytes=VMEM_LIMIT),
        cost_estimate=pl.CostEstimate(flops=flops, bytes_accessed=1 << 21, transcendentals=0),
    )(*args)


def contract(left, right):
    return lax.dot_general(left, right, (((0,), (0,)), ((), ())), preferred_element_type=F32)


def shards(
    orbital_block, cell_matrices, cell_nodes, shared_nodes, inv_sqrt_mass, potential, filter_center, filter_halfwidth
):
    band_count = lax.axis_size("band")
    dom_count = lax.axis_size("dom")
    planes = dom_count // GROUP
    nodes, width = orbital_block.shape
    cells = cell_matrices.shape[0]
    shared = shared_nodes.shape[1]
    rows = width // dom_count
    here = lax.axis_index("dom")
    band = lax.axis_index("band")
    plane, place = here // GROUP, here % GROUP
    place_arg = place.astype(jnp.int32).reshape(1)
    everyone = range(dom_count)

    def in_plane(block, k):
        return lax.ppermute(block, "dom", [(i, i ^ k) for i in everyone])

    def to_plane(block, k):
        route = [(i, (i // GROUP + k) % planes * GROUP + i % GROUP) for i in everyone]
        return lax.ppermute(block, "dom", route)

    def to_band(block, k):
        return lax.ppermute(block, "band", [(i, (i + k) % band_count) for i in range(band_count)])

    message = ((nodes + cells * LANES + EXTRA, LANES), BF16)
    messages = call(
        functools.partial(pack_kernel, planes),
        [message] * GROUP,
        (
            place_arg, orbital_block, cell_matrices, cell_nodes, shared_nodes,
            inv_sqrt_mass.reshape(-1, LANES), potential.reshape(-1, LANES),
        ),
        scalars=1,
        scratch=[pltpu.VMEM((LANES, LANES), F32)],
    )
    messages = [messages[0]] + [in_plane(messages[k], k) for k in range(1, GROUP)]
    height = GROUP * nodes
    column = ((height, LANES), F32)
    trace = ((FILTER_DEG * shared + 2 * shared, LANES), BF16)
    own, down, up, mass, scale, diag, start, next_msg, previous_msg = call(
        functools.partial(first_kernel, cells, shared),
        [
            ((GROUP, nodes, nodes), BF16), ((GROUP, 2 * shared, nodes), BF16), ((GROUP, nodes, 2 * shared), BF16),
            column, column, column, ((height, LANES), BF16), trace, trace,
        ],
        (place_arg, filter_center, filter_halfwidth, *messages),
        scalars=3,
        scratch=[
            pltpu.VMEM((GROUP, nodes, nodes), F32), pltpu.VMEM((GROUP, shared, shared), F32),
            pltpu.VMEM((height, 2 * LANES), F32), pltpu.VMEM((height, 2 * LANES), F32),
        ],
        flops=1 << 30,
    )
    below = to_plane(next_msg, 1)
    above = to_plane(previous_msg, -1)
    mine, next_msg, previous_msg = call(
        functools.partial(second_kernel, shared),
        [((height, LANES), BF16), ((shared, LANES), BF16), ((shared, LANES), BF16)],
        (own, down, up, mass, scale, diag, start, next_msg, below, above),
        scratch=[pltpu.VMEM((height, LANES), F32), pltpu.VMEM((height, LANES), F32)],
        flops=1 << 30,
    )
    below_now = to_plane(next_msg, 1)
    above_now = to_plane(previous_msg, -1)
    others = [in_plane(mine, k) for k in range(1, GROUP)]
    (applied,) = call(
        functools.partial(third_kernel, shared),
        [((height, LANES), BF16)],
        (filter_center, filter_halfwidth, own, down, up, mass, diag, mine, below, below_now, above_now),
        scalars=2,
        flops=1 << 28,
    )

    lefts = [applied] + [to_band(applied, k) for k in range(1, band_count)]
    lefts += [mine] + [to_band(mine, k) for k in range(1, band_count)]
    left = jnp.concatenate(lefts, axis=1)
    right = jnp.concatenate([mine] + others, axis=1)
    product = contract(left, right).reshape(2 * band_count, planes, rows, width)

    def part_for(k):
        return lax.dynamic_index_in_dim(product, (plane + k) % planes, 1, keepdims=False)

    total = part_for(0)
    for k in range(1, planes):
        total = total + to_plane(part_for(k).astype(BF16), k).astype(F32)

    total = total.reshape(2, band_count, rows, width)
    own_rows = total[:, 0]
    pieces = [own_rows] + [to_band(total[:, j], -j) for j in range(1, band_count)]
    stacked = jnp.stack(pieces)
    stacked = stacked.reshape(band_count, 2, rows, GROUP, LANES)
    ordered = jnp.stack(
        [
            jnp.stack([
                lax.dynamic_index_in_dim(
                    lax.dynamic_index_in_dim(stacked, (b - band) % band_count, 0, keepdims=False),
                    place ^ c, 2, keepdims=False,
                )
                for c in range(GROUP)
            ], axis=2)
            for b in range(band_count)
        ],
        axis=2,
    )
    ordered = ordered.reshape(2, rows, band_count, GROUP, planes, rows)
    ordered = jnp.transpose(ordered, (0, 1, 2, 4, 3, 5)).reshape(2, rows, band_count * width)
    factor = 1.0 / (nodes * dom_count)
    outcome = ordered * factor

    chunks = jnp.stack([mine] + others).reshape(GROUP, GROUP, nodes, LANES)
    chunks = lax.dynamic_index_in_dim(chunks, place, 1, keepdims=False)
    chunks = jnp.stack(
        [lax.dynamic_index_in_dim(chunks, place ^ c, 0, keepdims=False) for c in range(GROUP)], axis=1
    )
    chunks = chunks.reshape(nodes, GROUP, planes, rows)
    filtered = jnp.transpose(chunks, (0, 2, 1, 3)).reshape(nodes, width)
    return filtered, outcome[1], outcome[0]


def solution(mesh):
    return jax.shard_map(
        shards,
        mesh=mesh,
        in_specs=(
            P("dom", "band"),
            P("dom", None, None),
            P(None, "dom"),
            P("dom", None),
            P("dom"),
            P("dom"),
            P(),
            P(),
        ),
        out_specs=(P("dom", "band"), P(("band", "dom"), None), P(("band", "dom"), None)),
        check_vma=False,
    )
```

```python
import functools

import jax
import jax.numpy as jnp
from jax import lax
from jax.experimental import pallas as pl
from jax.experimental.pallas import tpu as pltpu
from jax.sharding import PartitionSpec as P

FILTER_DEG = 4
GROUP = 4
LANES = 128
EXTRA = 32
F32 = jnp.float32
BF16 = jnp.bfloat16
VMEM_LIMIT = 20 * 1024 * 1024


def dot(a, b):
    return jnp.dot(a, b, preferred_element_type=F32)


def dot_nt(a, b):
    return lax.dot_general(a, b, (((1,), (1,)), ((), ())), preferred_element_type=F32)


def iota(shape, dim):
    return lax.broadcasted_iota(jnp.int32, shape, dim)


def split3(x):
    high = x.astype(BF16)
    rest = x - high.astype(F32)
    middle = rest.astype(BF16)
    low = (rest - middle.astype(F32)).astype(BF16)
    return high, middle, low


def pack_kernel(planes, corners, place_ref, field_ref, cells_ref, small_ref, *refs):
    out_refs, square = refs[:GROUP], refs[GROUP]
    place = place_ref[0]
    nodes, width = field_ref.shape
    cells = cells_ref.shape[0]
    rows = LANES // planes
    line, lane = iota((LANES, LANES), 0), iota((LANES, LANES), 1)
    square[...] = jnp.zeros_like(square)
    for c in range(cells):
        square[c, 0:corners, 0:corners] = cells_ref[c].astype(F32)
    for c in range(0, cells, 2):
        first = square[c]
        second = square[c + 1] if c + 1 < cells else jnp.zeros_like(first)
        diagonal = 0.5 * jnp.sum(jnp.where(line == lane, second, 0.0), axis=0, keepdims=True)
        packed = jnp.where(line < lane, first, jnp.where(line > lane, second, 0.5 * first))
        packed = jnp.where(line == LANES - 1, diagonal, packed)
        for out in out_refs:
            out[nodes + c // 2 * LANES : nodes + (c // 2 + 1) * LANES, :] = packed.astype(BF16)
    small = small_ref[...]
    ids = small[0:cells, 0:LANES]
    high = jnp.floor(ids * (1.0 / 64.0))
    pieces = [high, ids - 64.0 * high, small[cells : cells + 1, 0:LANES]]
    for j in (1, 2):
        for part in split3(small[cells + j : cells + j + 1]):
            pieces += [part[:, h * LANES : (h + 1) * LANES].astype(F32) for h in range(nodes // LANES)]
    used = sum(piece.shape[0] for piece in pieces)
    pieces.append(jnp.zeros((EXTRA - used, LANES), F32))
    for out in out_refs:
        out[nodes + (cells + 1) // 2 * LANES :, :] = jnp.concatenate(pieces, axis=0).astype(BF16)
    source = iota((width, LANES), 0)
    target = iota((width, LANES), 1)
    wanted = (target // rows) * (GROUP * rows) + target % rows
    for k in range(GROUP):
        pick = wanted + (place ^ k) * rows == source
        out_refs[k][0:nodes, :] = dot(field_ref[...], pick.astype(F32).astype(BF16)).astype(BF16)


def apply_plane(own, down, up, fields, outside_u, outside_g, keep=None):
    shared = down[0].shape[0] // 2
    traces = [dot(down[i], fields[i]) for i in range(GROUP)]
    to_next = traces[GROUP - 1][:shared]
    to_previous = traces[0][shared:]
    w, g = outside_u, outside_g
    if callable(outside_u):
        w, g = outside_u(to_previous, to_next)
    sums = []
    for i in range(GROUP):
        if keep is not None and i not in keep:
            sums.append(None)
            continue
        below = w if i == 0 else traces[i - 1][:shared]
        above = g if i == GROUP - 1 else traces[i + 1][shared:]
        total = dot(own[i], fields[i])
        if below is None:
            below = jnp.zeros_like(to_next)
        if above is None:
            above = jnp.zeros_like(to_next)
        sides = jnp.concatenate([above, below], axis=0).astype(BF16)
        sums.append(total + dot(up[i], sides))
    return sums, traces


def build_kernel(
    nodes, cells, corners, shared, center_ref, half_ref, ref, own_ref, corner_ref, up_ref, down_ref, mass_ref, scale_ref, diag_ref,
):
    center, half = center_ref[0], half_ref[0]
    both = nodes + shared
    halves = nodes // LANES
    base = nodes + (cells + 1) // 2 * LANES
    line, lane = iota((LANES, LANES), 0), iota((LANES, LANES), 1)
    nothing = jnp.zeros((LANES, LANES), F32)
    extra = ref[base : base + EXTRA, :].astype(F32)
    ids = (64.0 * extra[0:cells] + extra[cells : 2 * cells]).astype(jnp.int32)
    picks, parts = [], []
    for c in range(cells):
        square = ref[nodes + c // 2 * LANES : nodes + (c // 2 + 1) * LANES, :].astype(F32)
        if c % 2 == 0:
            matrix = jnp.where(line <= lane, square, nothing)
        else:
            matrix = jnp.where((line > lane) & (line < corners), square, nothing)
            matrix = matrix + jnp.where(line == lane, square[LANES - 1 :], nothing)
        pick = (iota((both, LANES), 0) == ids[c : c + 1]).astype(F32).astype(BF16)
        picks.append(pick)
        parts.append(dot(pick, matrix.astype(BF16)).astype(BF16))
    total = dot_nt(jnp.concatenate(parts + picks, axis=1), jnp.concatenate(picks + parts, axis=1))
    own_ref[...] = total[:nodes, :nodes]
    corner_ref[...] = total[nodes:, nodes:]
    own_shared = extra[2 * cells : 2 * cells + 1, 0:shared].astype(jnp.int32)
    place_in = (iota((nodes, shared), 0) == own_shared).astype(F32)
    sides = jnp.concatenate([total[:nodes, nodes:], place_in], axis=1)
    up_ref[...] = sides.astype(BF16)
    down_ref[...] = jnp.transpose(sides).astype(BF16)
    row = 2 * cells + 1
    for h in range(halves):
        at = slice(h * LANES, (h + 1) * LANES)
        mass_row = sum(extra[row + j * halves + h : row + j * halves + h + 1] for j in range(3))
        off = row + 3 * halves
        pot_row = sum(extra[off + j * halves + h : off + j * halves + h + 1] for j in range(3))
        mass = jnp.transpose(jnp.broadcast_to(mass_row, (LANES, LANES)))
        pot = jnp.transpose(jnp.broadcast_to(pot_row, (LANES, LANES)))
        mass_ref[at, :] = mass
        scale_ref[at, :] = mass / half
        diag_ref[at, :] = (pot - center) / half


def first_kernel(shared, place_ref, *refs):
    messages, refs = refs[:GROUP], refs[GROUP:]
    slabs = [refs[7 * k : 7 * k + 7] for k in range(GROUP)]
    own_ref, down_ref, up_ref, mass_ref, scale_ref, diag_ref, start_ref = refs[7 * GROUP : 7 * GROUP + 7]
    next_ref, previous_ref, raw, corner, cur, prev = refs[7 * GROUP + 7 :]
    place = place_ref[0]
    nodes = own_ref.shape[1]
    for k in range(GROUP):
        slab = place ^ k
        at = pl.ds(pl.multiple_of(slab * nodes, nodes), nodes)
        own_k, corner_k, up_k, down_k, mass_k, scale_k, diag_k = slabs[k]
        start_ref[at, :] = messages[k][0:nodes, :]
        raw[slab] = own_k[...]
        corner[slab] = corner_k[...]
        up_ref[slab] = up_k[...]
        down_ref[slab] = down_k[...]
        mass_ref[at, :] = mass_k[...]
        scale_ref[at, :] = scale_k[...]
        diag_ref[at, :] = diag_k[...]
    own_ref[0] = raw[0].astype(BF16)
    for i in range(1, GROUP):
        place_in = up_ref[i][:, shared:]
        moved = dot(place_in, corner[i - 1].astype(BF16)).astype(BF16)
        own_ref[i] = (raw[i] + dot_nt(moved, place_in)).astype(BF16)

    cur[:, 0:LANES] = start_ref[...].astype(F32)
    cur[:, LANES:] = jnp.zeros((GROUP * nodes, 2 * shared), F32)
    top = (GROUP - 1) * nodes
    first = up_ref[0].astype(F32)
    last = up_ref[GROUP - 1].astype(F32)
    lane = iota((nodes, 2 * shared), 1)
    swapped = jnp.concatenate([first[:, shared:], first[:, :shared]], axis=1)
    cur[0:nodes, LANES:] = jnp.where(lane < shared, swapped * scale_ref[0:nodes, :], 0.0)
    swapped = jnp.concatenate([last[:, shared:], last[:, :shared]], axis=1)
    cur[top:, LANES:] = cur[top:, LANES:] + jnp.where(lane >= shared, swapped * scale_ref[top:, :], 0.0)
    prev[...] = jnp.zeros_like(prev)

    own = [own_ref[i] for i in range(GROUP)]
    down = [down_ref[i] for i in range(GROUP)]
    up = [up_ref[i] for i in range(GROUP)]

    def wide(ref, i):
        part = ref[i * nodes : (i + 1) * nodes, :]
        return jnp.concatenate([part, part], axis=1)

    next_parts, previous_parts = [], []
    for k in range(FILTER_DEG):
        last_step = k == FILTER_DEG - 1
        if last_step:
            field0 = (mass_ref[0:nodes, :] * cur[0:nodes, 0:LANES]).astype(BF16)
            field3 = (mass_ref[top:, :] * cur[top:, 0:LANES]).astype(BF16)
            next_ref[k * shared : (k + 1) * shared, :] = dot(down[GROUP - 1], field3)[:shared].astype(BF16)
            previous_ref[k * shared : (k + 1) * shared, :] = dot(down[0], field0)[shared:].astype(BF16)
            break
        fields = [(wide(mass_ref, i) * cur[i * nodes : (i + 1) * nodes, :]).astype(BF16) for i in range(GROUP)]
        keep = None if k < FILTER_DEG - 2 else (0, GROUP - 1)
        sums, traces = apply_plane(own, down, up, fields, None, None, keep)
        to_next = traces[GROUP - 1][:shared]
        to_previous = traces[0][shared:]
        next_ref[k * shared : (k + 1) * shared, :] = to_next[:, 0:LANES].astype(BF16)
        previous_ref[k * shared : (k + 1) * shared, :] = to_previous[:, 0:LANES].astype(BF16)
        next_parts.append(to_next[:, LANES + shared :])
        previous_parts.append(to_previous[:, LANES : LANES + shared])
        for i in range(GROUP):
            if sums[i] is None:
                continue
            at = slice(i * nodes, (i + 1) * nodes)
            now = cur[at, :]
            image = wide(scale_ref, i) * sums[i] + wide(diag_ref, i) * now
            if k == 0:
                factor = jnp.where(iota((1, 2 * LANES), 1) < LANES, 1.0, 2.0)
                new = factor * image
            else:
                new = 2.0 * image - prev[at, :]
            prev[at, :] = now
            cur[at, :] = new
    at = FILTER_DEG * shared
    next_parts.append(corner[GROUP - 1])
    previous_parts.append(jnp.zeros((shared, shared), F32))
    for j in range(2):
        next_ref[at + j * shared : at + (j + 1) * shared, :] = jnp.concatenate(
            next_parts[2 * j : 2 * j + 2], axis=1
        ).astype(BF16)
        previous_ref[at + j * shared : at + (j + 1) * shared, :] = jnp.concatenate(
            previous_parts[2 * j : 2 * j + 2], axis=1
        ).astype(BF16)


def second_kernel(
    shared, own_ref, down_ref, up_ref, mass_ref, scale_ref, diag_ref, start_ref, sent_ref, below_ref, above_ref,
    filtered_ref, next_ref, previous_ref, cur, prev,
):
    nodes = own_ref.shape[1]
    own = [own_ref[i] for i in range(GROUP)]
    down = [down_ref[i] for i in range(GROUP)]
    up = [up_ref[i] for i in range(GROUP)]
    at = FILTER_DEG * shared
    near_b, far_b = below_ref[at : at + shared, :], below_ref[at + shared : at + 2 * shared, :]
    near_a, far_a = above_ref[at : at + shared, :], above_ref[at + shared : at + 2 * shared, :]
    mine = sent_ref[at + shared : at + 2 * shared, :]
    zero = jnp.zeros((shared, LANES), BF16)
    cur[...] = start_ref[...].astype(F32)
    prev[...] = jnp.zeros_like(prev)
    below_past, above_past = [], []

    def past(items, lag):
        if lag > len(items):
            return zero
        item = items[len(items) - lag]
        return item if lag == len(items) else item * 2

    def pair(a, b):
        return jnp.concatenate([a, b], axis=0)

    for k in range(FILTER_DEG):

        def outside(to_previous, to_next, k=k):
            here = to_previous.astype(BF16)
            below = below_ref[k * shared : (k + 1) * shared, :].astype(F32)
            below = below + dot(near_b, pair(past(below_past, 1), past(below_past, 2)))
            below = below + dot(far_b, pair(past(below_past, 3), here))
            above = above_ref[k * shared : (k + 1) * shared, :].astype(F32)
            above = above + dot(near_a, pair(past(above_past, 1), past(above_past, 2)))
            above = above + dot(far_a, pair(past(above_past, 3), zero))
            force = to_next + dot(mine, pair(zero, above.astype(BF16)))
            below_past.append(here)
            above_past.append(force.astype(BF16))
            return below, above

        fields = [
            (mass_ref[i * nodes : (i + 1) * nodes, :] * cur[i * nodes : (i + 1) * nodes, :]).astype(BF16)
            for i in range(GROUP)
        ]
        sums, _ = apply_plane(own, down, up, fields, outside, None)
        for i in range(GROUP):
            rows = slice(i * nodes, (i + 1) * nodes)
            now = cur[rows, :]
            image = scale_ref[rows, :] * sums[i] + diag_ref[rows, :] * now
            new = image if k == 0 else 2.0 * image - prev[rows, :]
            prev[rows, :] = now
            cur[rows, :] = new
    filtered_ref[...] = cur[...].astype(BF16)
    top = (GROUP - 1) * nodes
    field0 = (mass_ref[0:nodes, :] * filtered_ref[0:nodes, :].astype(F32)).astype(BF16)
    field3 = (mass_ref[top:, :] * filtered_ref[top:, :].astype(F32)).astype(BF16)
    next_ref[...] = dot(down[GROUP - 1], field3)[:shared].astype(BF16)
    previous_ref[...] = dot(down[0], field0)[shared:].astype(BF16)


def third_kernel(
    shared, center_ref, half_ref, own_ref, down_ref, up_ref, mass_ref, diag_ref, filtered_ref, corner_ref, below_ref,
    above_ref, applied_ref,
):
    nodes = own_ref.shape[1]
    center, half = center_ref[0], half_ref[0]
    own = [own_ref[i] for i in range(GROUP)]
    down = [down_ref[i] for i in range(GROUP)]
    up = [up_ref[i] for i in range(GROUP)]
    at = FILTER_DEG * shared
    far_b = corner_ref[at + shared : at + 2 * shared, :]
    zero = jnp.zeros((shared, LANES), BF16)

    def outside(to_previous, to_next):
        below = below_ref[...].astype(F32)
        below = below + dot(far_b, jnp.concatenate([zero, to_previous.astype(BF16)], axis=0))
        return below, above_ref[...].astype(F32)

    values = [filtered_ref[i * nodes : (i + 1) * nodes, :].astype(F32) for i in range(GROUP)]
    fields = [(mass_ref[i * nodes : (i + 1) * nodes, :] * values[i]).astype(BF16) for i in range(GROUP)]
    sums, _ = apply_plane(own, down, up, fields, outside, None)
    for i in range(GROUP):
        rows = slice(i * nodes, (i + 1) * nodes)
        pot = diag_ref[rows, :] * half + center
        applied_ref[rows, :] = (mass_ref[rows, :] * sums[i] + pot * values[i]).astype(BF16)


SPACES = {"s": pltpu.SMEM, "v": pltpu.VMEM, "a": pl.ANY}


def call(kernel, outs, args, spaces=None, scratch=(), flops=0):
    spaces = spaces or "v" * len(args)
    return pl.pallas_call(
        kernel,
        out_shape=[jax.ShapeDtypeStruct(shape, dtype) for shape, dtype in outs],
        in_specs=[pl.BlockSpec(memory_space=SPACES[space]) for space in spaces],
        out_specs=[pl.BlockSpec(memory_space=pltpu.VMEM)] * len(outs),
        scratch_shapes=list(scratch),
        compiler_params=pltpu.CompilerParams(vmem_limit_bytes=VMEM_LIMIT),
        cost_estimate=pl.CostEstimate(flops=flops, bytes_accessed=1 << 21, transcendentals=0),
    )(*args)


def place_kernel(planes, factor, place_ref, band_ref, *refs):
    pieces, outs = refs[:-2], refs[-2:]
    place, band = place_ref[0], band_ref[0]
    _, rows, width = pieces[0].shape
    bands = len(pieces)
    for j, piece in enumerate(pieces):
        first = ((band + j) % bands) * width
        for mat, out in enumerate(outs):
            chunks = [
                piece[mat, :, pl.ds(pl.multiple_of((place ^ c) * LANES, LANES), LANES)] * factor for c in range(GROUP)
            ]
            columns = [
                jnp.concatenate([chunk[:, z * rows : (z + 1) * rows] for chunk in chunks], axis=1)
                for z in range(planes)
            ]
            out[:, pl.ds(pl.multiple_of(first, LANES), width)] = jnp.concatenate(columns, axis=1)


def contract(left, right):
    return lax.dot_general(left, right, (((0,), (0,)), ((), ())), preferred_element_type=F32)


def shards(
    orbital_block, cell_matrices, cell_nodes, shared_nodes, inv_sqrt_mass, potential, filter_center, filter_halfwidth
):
    band_count = lax.axis_size("band")
    dom_count = lax.axis_size("dom")
    planes = dom_count // GROUP
    nodes, width = orbital_block.shape
    cells, corners, _ = cell_matrices.shape
    shared = shared_nodes.shape[1]
    rows = width // dom_count
    here = lax.axis_index("dom")
    band = lax.axis_index("band")
    plane, place = here // GROUP, here % GROUP
    place_arg = place.astype(jnp.int32).reshape(1)
    everyone = range(dom_count)

    def in_plane(block, k):
        return lax.ppermute(block, "dom", [(i, i ^ k) for i in everyone])

    def to_plane(block, k):
        route = [(i, (i // GROUP + k) % planes * GROUP + i % GROUP) for i in everyone]
        return lax.ppermute(block, "dom", route)

    def partner(index, k):
        return index ^ k if planes & (planes - 1) == 0 else (2 * planes + k - index) % planes

    def to_band(block, k):
        return lax.ppermute(block, "band", [(i, (i + k) % band_count) for i in range(band_count)])

    def line(values, fill):
        return jnp.pad(values.astype(F32), ((0, 0), (0, nodes - values.shape[1])), constant_values=fill)

    small = jnp.concatenate(
        [line(cell_nodes.T, -512.0), line(shared_nodes, 0.0), inv_sqrt_mass[None], potential[None]], axis=0
    )
    messages = call(
        functools.partial(pack_kernel, planes, corners),
        [((nodes + (cells + 1) // 2 * LANES + EXTRA, LANES), BF16)] * GROUP,
        (place_arg, orbital_block, cell_matrices, small),
        spaces="svvv",
        scratch=[pltpu.VMEM((cells, LANES, LANES), F32)],
    )
    messages = [messages[0]] + [in_plane(messages[k], k) for k in range(1, GROUP)]
    slabs = []
    for message in messages:
        slabs += call(
            functools.partial(build_kernel, nodes, cells, corners, shared),
            [
                ((nodes, nodes), F32), ((shared, shared), F32), ((nodes, 2 * shared), BF16), ((2 * shared, nodes), BF16),
            ] + [((nodes, LANES), F32)] * 3,
            (filter_center, filter_halfwidth, message),
            spaces="ssv",
            flops=1 << 28,
        )
    height = GROUP * nodes
    column = ((height, LANES), F32)
    trace = ((FILTER_DEG * shared + 2 * shared, LANES), BF16)
    own, down, up, mass, scale, diag, start, next_msg, previous_msg = call(
        functools.partial(first_kernel, shared),
        [
            ((GROUP, nodes, nodes), BF16), ((GROUP, 2 * shared, nodes), BF16), ((GROUP, nodes, 2 * shared), BF16),
            column, column, column, ((height, LANES), BF16), trace, trace,
        ],
        (place_arg, *messages, *slabs),
        spaces="s" + "v" * (GROUP * 8),
        scratch=[
            pltpu.VMEM((GROUP, nodes, nodes), F32), pltpu.VMEM((GROUP, shared, shared), F32),
            pltpu.VMEM((height, 2 * LANES), F32), pltpu.VMEM((height, 2 * LANES), F32),
        ],
        flops=1 << 30,
    )
    below = to_plane(next_msg, 1)
    above = to_plane(previous_msg, -1)
    mine, next_msg, previous_msg = call(
        functools.partial(second_kernel, shared),
        [((height, LANES), BF16), ((shared, LANES), BF16), ((shared, LANES), BF16)],
        (own, down, up, mass, scale, diag, start, next_msg, below, above),
        scratch=[pltpu.VMEM((height, LANES), F32), pltpu.VMEM((height, LANES), F32)],
        flops=1 << 30,
    )
    below_now = to_plane(next_msg, 1)
    above_now = to_plane(previous_msg, -1)
    others = [in_plane(mine, k) for k in range(1, GROUP)]
    (applied,) = call(
        functools.partial(third_kernel, shared),
        [((height, LANES), BF16)],
        (filter_center, filter_halfwidth, own, down, up, mass, diag, mine, below, below_now, above_now),
        spaces="ss" + "v" * 9,
        flops=1 << 28,
    )

    applied, mine, *others = lax.optimization_barrier((applied, mine, *others))
    lefts = [applied] + [to_band(applied, k) for k in range(1, band_count)]
    lefts += [mine] + [to_band(mine, k) for k in range(1, band_count)]
    left = jnp.concatenate(lefts, axis=1)
    gathered = [mine] + others
    totals = []
    for part in ((0, 1, 2, 3),):
        right = gathered[part[0]] if len(part) == 1 else jnp.concatenate([gathered[k] for k in part], axis=1)
        product = contract(left, right).reshape(2 * band_count, planes, rows, len(part) * LANES)

        def part_for(k, product=product):
            return lax.dynamic_index_in_dim(product, partner(plane, k), 1, keepdims=False)

        total = part_for(0)
        for k in [*range(2, planes), 1]:
            route = [(i, partner(i // GROUP, k) * GROUP + i % GROUP) for i in everyone]
            total = total + lax.ppermute(part_for(k).astype(BF16), "dom", route).astype(F32)
        totals.append(total)
    total = jnp.concatenate(totals, axis=2).reshape(2, band_count, rows, width)
    pieces = [total[:, 0]] + [to_band(total[:, j], -j) for j in range(1, band_count)]
    projected, intersection = call(
        functools.partial(place_kernel, planes, 1.0 / (nodes * dom_count)),
        [((rows, band_count * width), F32)] * 2,
        (place_arg, band.astype(jnp.int32).reshape(1), *pieces),
        spaces="ss" + "v" * band_count,
    )
    chunks = jnp.stack([mine] + others).reshape(GROUP, GROUP, nodes, LANES)
    chunks = lax.dynamic_index_in_dim(chunks, place, 1, keepdims=False)
    chunks = jnp.stack(
        [lax.dynamic_index_in_dim(chunks, place ^ c, 0, keepdims=False) for c in range(GROUP)], axis=1
    )
    chunks = chunks.reshape(nodes, GROUP, planes, rows)
    filtered = jnp.transpose(chunks, (0, 2, 1, 3)).reshape(nodes, width)
    return filtered, intersection, projected


def solution(mesh):
    return jax.shard_map(
        shards,
        mesh=mesh,
        in_specs=(
            P("dom", "band"),
            P("dom", None, None),
            P(None, "dom"),
            P("dom", None),
            P("dom"),
            P("dom"),
            P(),
            P(),
        ),
        out_specs=(P("dom", "band"), P(("band", "dom"), None), P(("band", "dom"), None)),
        check_vma=False,
    )
```

```python
import functools

import jax
import jax.numpy as jnp
from jax import lax
from jax.experimental import pallas as pl
from jax.experimental.pallas import tpu as pltpu
from jax.sharding import PartitionSpec as P

FILTER_DEG = 4
GROUP = 4
LANES = 128
EXTRA = 32
F32 = jnp.float32
BF16 = jnp.bfloat16
VMEM_LIMIT = 20 * 1024 * 1024


def dot(a, b):
    return jnp.dot(a, b, preferred_element_type=F32)


def dot_nt(a, b):
    return lax.dot_general(a, b, (((1,), (1,)), ((), ())), preferred_element_type=F32)


def iota(shape, dim):
    return lax.broadcasted_iota(jnp.int32, shape, dim)


def split3(x):
    high = x.astype(BF16)
    rest = x - high.astype(F32)
    middle = rest.astype(BF16)
    low = (rest - middle.astype(F32)).astype(BF16)
    return high, middle, low


def pack_kernel(planes, corners, place_ref, field_ref, cells_ref, small_ref, *refs):
    out_refs, square = refs[:GROUP], refs[GROUP]
    place = place_ref[0]
    nodes, width = field_ref.shape
    cells = cells_ref.shape[0]
    rows = LANES // planes
    line, lane = iota((LANES, LANES), 0), iota((LANES, LANES), 1)
    square[...] = jnp.zeros_like(square)
    for c in range(cells):
        square[c, 0:corners, 0:corners] = cells_ref[c].astype(F32)
    for c in range(0, cells, 2):
        first = square[c]
        second = square[c + 1] if c + 1 < cells else jnp.zeros_like(first)
        diagonal = 0.5 * jnp.sum(jnp.where(line == lane, second, 0.0), axis=0, keepdims=True)
        packed = jnp.where(line < lane, first, jnp.where(line > lane, second, 0.5 * first))
        packed = jnp.where(line == LANES - 1, diagonal, packed)
        for out in out_refs:
            out[nodes + c // 2 * LANES : nodes + (c // 2 + 1) * LANES, :] = packed.astype(BF16)
    small = small_ref[...]
    ids = small[0:cells, 0:LANES]
    high = jnp.floor(ids * (1.0 / 64.0))
    high = jnp.where(iota((cells, LANES), 1) < corners, high, -8.0)
    pieces = [high, ids - 64.0 * jnp.maximum(high, 0.0), small[cells : cells + 1, 0:LANES]]
    for j in (1, 2):
        for part in split3(small[cells + j : cells + j + 1]):
            pieces += [part[:, h * LANES : (h + 1) * LANES].astype(F32) for h in range(nodes // LANES)]
    used = sum(piece.shape[0] for piece in pieces)
    pieces.append(jnp.zeros((EXTRA - used, LANES), F32))
    for out in out_refs:
        out[nodes + (cells + 1) // 2 * LANES :, :] = jnp.concatenate(pieces, axis=0).astype(BF16)
    source = iota((width, LANES), 0)
    target = iota((width, LANES), 1)
    wanted = (target // rows) * (GROUP * rows) + target % rows
    for k in range(GROUP):
        pick = wanted + (place ^ k) * rows == source
        out_refs[k][0:nodes, :] = dot(field_ref[...], pick.astype(F32).astype(BF16)).astype(BF16)


def apply_plane(own, down, up, fields, outside_u, outside_g, keep=None):
    shared = down[0].shape[0] // 2
    traces = [dot(down[i], fields[i]) for i in range(GROUP)]
    to_next = traces[GROUP - 1][:shared]
    to_previous = traces[0][shared:]
    w, g = outside_u, outside_g
    if callable(outside_u):
        w, g = outside_u(to_previous, to_next)
    sums = []
    for i in range(GROUP):
        if keep is not None and i not in keep:
            sums.append(None)
            continue
        below = w if i == 0 else traces[i - 1][:shared]
        above = g if i == GROUP - 1 else traces[i + 1][shared:]
        total = dot(own[i], fields[i])
        if below is None:
            below = jnp.zeros_like(to_next)
        if above is None:
            above = jnp.zeros_like(to_next)
        sides = jnp.concatenate([above, below], axis=0).astype(BF16)
        sums.append(total + dot(up[i], sides))
    return sums, traces


def build_kernel(
    nodes, cells, corners, shared, center_ref, half_ref, ref, _, own_ref, corner_ref, up_ref, down_ref, mass_ref, scale_ref, diag_ref,
):
    center, half = center_ref[0], half_ref[0]
    both = nodes + shared
    halves = nodes // LANES
    base = nodes + (cells + 1) // 2 * LANES
    line, lane = iota((LANES, LANES), 0), iota((LANES, LANES), 1)
    nothing = jnp.zeros((LANES, LANES), F32)
    extra = ref[base : base + EXTRA, :].astype(F32)
    ids = (64.0 * extra[0:cells] + extra[cells : 2 * cells]).astype(jnp.int32)
    picks, parts = [], []
    for c in range(cells):
        square = ref[nodes + c // 2 * LANES : nodes + (c // 2 + 1) * LANES, :].astype(F32)
        if c % 2 == 0:
            matrix = jnp.where(line <= lane, square, nothing)
        else:
            matrix = jnp.where((line > lane) & (line < corners), square, nothing)
            matrix = matrix + jnp.where(line == lane, square[LANES - 1 :], nothing)
        pick = (iota((both, LANES), 0) == ids[c : c + 1]).astype(F32).astype(BF16)
        picks.append(pick)
        parts.append(dot(pick, matrix.astype(BF16)).astype(BF16))
    total = dot_nt(jnp.concatenate(parts + picks, axis=1), jnp.concatenate(picks + parts, axis=1))
    own_ref[...] = total[:nodes, :nodes]
    corner_ref[...] = total[nodes:, nodes:]
    own_shared = extra[2 * cells : 2 * cells + 1, 0:shared].astype(jnp.int32)
    place_in = (iota((nodes, shared), 0) == own_shared).astype(F32)
    sides = jnp.concatenate([total[:nodes, nodes:], place_in], axis=1)
    up_ref[...] = sides.astype(BF16)
    down_ref[...] = jnp.transpose(sides).astype(BF16)
    row = 2 * cells + 1
    for h in range(halves):
        at = slice(h * LANES, (h + 1) * LANES)
        mass_row = sum(extra[row + j * halves + h : row + j * halves + h + 1] for j in range(3))
        off = row + 3 * halves
        pot_row = sum(extra[off + j * halves + h : off + j * halves + h + 1] for j in range(3))
        mass = jnp.transpose(jnp.broadcast_to(mass_row, (LANES, LANES)))
        pot = jnp.transpose(jnp.broadcast_to(pot_row, (LANES, LANES)))
        mass_ref[at, :] = mass
        scale_ref[at, :] = mass / half
        diag_ref[at, :] = (pot - center) / half


def first_kernel(shared, place_ref, odd_ref, *refs):
    messages, refs = refs[:GROUP], refs[GROUP:]
    slabs = [refs[7 * k : 7 * k + 7] for k in range(GROUP)]
    own_ref, down_ref, up_ref, mass_ref, scale_ref, diag_ref, start_ref = refs[7 * GROUP : 7 * GROUP + 7]
    keep_ref, pair0_ref, pair1_ref, raw, corner, cur, prev, box = refs[7 * GROUP + 7 :]
    next_ref, previous_ref = box.at[0], box.at[1]
    place = place_ref[0]
    nodes = own_ref.shape[1]
    for k in range(GROUP):
        slab = place ^ k
        at = pl.ds(pl.multiple_of(slab * nodes, nodes), nodes)
        own_k, corner_k, up_k, down_k, mass_k, scale_k, diag_k = slabs[k]
        start_ref[at, :] = messages[k][0:nodes, :]
        raw[slab] = own_k[...]
        corner[slab] = corner_k[...]
        up_ref[slab] = up_k[...]
        down_ref[slab] = down_k[...]
        mass_ref[at, :] = mass_k[...]
        scale_ref[at, :] = scale_k[...]
        diag_ref[at, :] = diag_k[...]
    own_ref[0] = raw[0].astype(BF16)
    for i in range(1, GROUP):
        place_in = up_ref[i][:, shared:]
        moved = dot(place_in, corner[i - 1].astype(BF16)).astype(BF16)
        own_ref[i] = (raw[i] + dot_nt(moved, place_in)).astype(BF16)

    cur[:, 0:LANES] = start_ref[...].astype(F32)
    cur[:, LANES:] = jnp.zeros((GROUP * nodes, 2 * shared), F32)
    top = (GROUP - 1) * nodes
    first = up_ref[0].astype(F32)
    last = up_ref[GROUP - 1].astype(F32)
    lane = iota((nodes, 2 * shared), 1)
    swapped = jnp.concatenate([first[:, shared:], first[:, :shared]], axis=1)
    cur[0:nodes, LANES:] = jnp.where(lane < shared, swapped * scale_ref[0:nodes, :], 0.0)
    swapped = jnp.concatenate([last[:, shared:], last[:, :shared]], axis=1)
    cur[top:, LANES:] = cur[top:, LANES:] + jnp.where(lane >= shared, swapped * scale_ref[top:, :], 0.0)
    prev[...] = jnp.zeros_like(prev)

    own = [own_ref[i] for i in range(GROUP)]
    down = [down_ref[i] for i in range(GROUP)]
    up = [up_ref[i] for i in range(GROUP)]

    def wide(ref, i):
        part = ref[i * nodes : (i + 1) * nodes, :]
        return jnp.concatenate([part, part], axis=1)

    next_parts, previous_parts = [], []
    for k in range(FILTER_DEG):
        last_step = k == FILTER_DEG - 1
        if last_step:
            field0 = (mass_ref[0:nodes, :] * cur[0:nodes, 0:LANES]).astype(BF16)
            field3 = (mass_ref[top:, :] * cur[top:, 0:LANES]).astype(BF16)
            next_ref[k * shared : (k + 1) * shared, :] = dot(down[GROUP - 1], field3)[:shared].astype(BF16)
            previous_ref[k * shared : (k + 1) * shared, :] = dot(down[0], field0)[shared:].astype(BF16)
            break
        fields = [(wide(mass_ref, i) * cur[i * nodes : (i + 1) * nodes, :]).astype(BF16) for i in range(GROUP)]
        keep = None if k < FILTER_DEG - 2 else (0, GROUP - 1)
        sums, traces = apply_plane(own, down, up, fields, None, None, keep)
        to_next = traces[GROUP - 1][:shared]
        to_previous = traces[0][shared:]
        next_ref[k * shared : (k + 1) * shared, :] = to_next[:, 0:LANES].astype(BF16)
        previous_ref[k * shared : (k + 1) * shared, :] = to_previous[:, 0:LANES].astype(BF16)
        next_parts.append(to_next[:, LANES + shared :])
        previous_parts.append(to_previous[:, LANES : LANES + shared])
        for i in range(GROUP):
            if sums[i] is None:
                continue
            at = slice(i * nodes, (i + 1) * nodes)
            now = cur[at, :]
            image = wide(scale_ref, i) * sums[i] + wide(diag_ref, i) * now
            if k == 0:
                factor = jnp.where(iota((1, 2 * LANES), 1) < LANES, 1.0, 2.0)
                new = factor * image
            else:
                new = 2.0 * image - prev[at, :]
            prev[at, :] = now
            cur[at, :] = new
    at = FILTER_DEG * shared
    next_parts.append(corner[GROUP - 1])
    previous_parts.append(jnp.zeros((shared, shared), F32))
    for j in range(2):
        next_ref[at + j * shared : at + (j + 1) * shared, :] = jnp.concatenate(
            next_parts[2 * j : 2 * j + 2], axis=1
        ).astype(BF16)
        previous_ref[at + j * shared : at + (j + 1) * shared, :] = jnp.concatenate(
            previous_parts[2 * j : 2 * j + 2], axis=1
        ).astype(BF16)
    keep_ref[...] = next_ref[at + shared : at + 2 * shared, :]
    odd = odd_ref[0]
    pair0_ref[...] = box[odd]
    pair1_ref[...] = box[1 - odd]


def second_kernel(
    shared, odd_ref, own_ref, down_ref, up_ref, mass_ref, scale_ref, diag_ref, start_ref, keep_ref, from0_ref, from1_ref,
    filtered_ref, corner_ref, pair0_ref, pair1_ref, cur, prev, box,
):
    odd = odd_ref[0]
    box[0] = from0_ref[...]
    box[1] = from1_ref[...]
    above_ref, below_ref = box.at[odd], box.at[1 - odd]
    nodes = own_ref.shape[1]
    own = [own_ref[i] for i in range(GROUP)]
    down = [down_ref[i] for i in range(GROUP)]
    up = [up_ref[i] for i in range(GROUP)]
    at = FILTER_DEG * shared
    near_b, far_b = below_ref[at : at + shared, :], below_ref[at + shared : at + 2 * shared, :]
    near_a, far_a = above_ref[at : at + shared, :], above_ref[at + shared : at + 2 * shared, :]
    mine = keep_ref[...]
    corner_ref[...] = far_b
    zero = jnp.zeros((shared, LANES), BF16)
    cur[...] = start_ref[...].astype(F32)
    prev[...] = jnp.zeros_like(prev)
    below_past, above_past = [], []

    def past(items, lag):
        if lag > len(items):
            return zero
        item = items[len(items) - lag]
        return item if lag == len(items) else item * 2

    def pair(a, b):
        return jnp.concatenate([a, b], axis=0)

    for k in range(FILTER_DEG):

        def outside(to_previous, to_next, k=k):
            here = to_previous.astype(BF16)
            below = below_ref[k * shared : (k + 1) * shared, :].astype(F32)
            below = below + dot(near_b, pair(past(below_past, 1), past(below_past, 2)))
            below = below + dot(far_b, pair(past(below_past, 3), here))
            above = above_ref[k * shared : (k + 1) * shared, :].astype(F32)
            above = above + dot(near_a, pair(past(above_past, 1), past(above_past, 2)))
            above = above + dot(far_a, pair(past(above_past, 3), zero))
            force = to_next + dot(mine, pair(zero, above.astype(BF16)))
            below_past.append(here)
            above_past.append(force.astype(BF16))
            return below, above

        fields = [
            (mass_ref[i * nodes : (i + 1) * nodes, :] * cur[i * nodes : (i + 1) * nodes, :]).astype(BF16)
            for i in range(GROUP)
        ]
        sums, _ = apply_plane(own, down, up, fields, outside, None)
        for i in range(GROUP):
            rows = slice(i * nodes, (i + 1) * nodes)
            now = cur[rows, :]
            image = scale_ref[rows, :] * sums[i] + diag_ref[rows, :] * now
            new = image if k == 0 else 2.0 * image - prev[rows, :]
            prev[rows, :] = now
            cur[rows, :] = new
    filtered_ref[...] = cur[...].astype(BF16)
    top = (GROUP - 1) * nodes
    field0 = (mass_ref[0:nodes, :] * filtered_ref[0:nodes, :].astype(F32)).astype(BF16)
    field3 = (mass_ref[top:, :] * filtered_ref[top:, :].astype(F32)).astype(BF16)
    box[0, 0:shared, :] = dot(down[GROUP - 1], field3)[:shared].astype(BF16)
    box[1, 0:shared, :] = dot(down[0], field0)[shared:].astype(BF16)
    pair0_ref[...] = box[odd, 0:shared, :]
    pair1_ref[...] = box[1 - odd, 0:shared, :]


def third_kernel(
    shared, odd_ref, center_ref, half_ref, own_ref, down_ref, up_ref, mass_ref, diag_ref, filtered_ref, corner_ref,
    from0_ref, from1_ref, left_ref, box,
):
    nodes = own_ref.shape[1]
    center, half = center_ref[0], half_ref[0]
    own = [own_ref[i] for i in range(GROUP)]
    down = [down_ref[i] for i in range(GROUP)]
    up = [up_ref[i] for i in range(GROUP)]
    odd = odd_ref[0]
    box[0] = from0_ref[...]
    box[1] = from1_ref[...]
    above_ref, below_ref = box.at[odd], box.at[1 - odd]
    far_b = corner_ref[...]
    zero = jnp.zeros((shared, LANES), BF16)

    def outside(to_previous, to_next):
        below = below_ref[...].astype(F32)
        below = below + dot(far_b, jnp.concatenate([zero, to_previous.astype(BF16)], axis=0))
        return below, above_ref[...].astype(F32)

    values = [filtered_ref[i * nodes : (i + 1) * nodes, :].astype(F32) for i in range(GROUP)]
    fields = [(mass_ref[i * nodes : (i + 1) * nodes, :] * values[i]).astype(BF16) for i in range(GROUP)]
    sums, _ = apply_plane(own, down, up, fields, outside, None)
    for i in range(GROUP):
        rows = slice(i * nodes, (i + 1) * nodes)
        pot = diag_ref[rows, :] * half + center
        applied = mass_ref[rows, :] * sums[i] + pot * values[i]
        left_ref[0:LANES, rows] = jnp.transpose(applied).astype(BF16)
        left_ref[LANES:, rows] = jnp.transpose(values[i]).astype(BF16)


SPACES = {"s": pltpu.SMEM, "v": pltpu.VMEM, "a": pl.ANY}


def call(kernel, outs, args, spaces=None, scratch=(), flops=0):
    spaces = spaces or "v" * len(args)
    return pl.pallas_call(
        kernel,
        out_shape=[jax.ShapeDtypeStruct(shape, dtype) for shape, dtype in outs],
        in_specs=[pl.BlockSpec(memory_space=SPACES[space]) for space in spaces],
        out_specs=[pl.BlockSpec(memory_space=pltpu.VMEM)] * len(outs),
        scratch_shapes=list(scratch),
        compiler_params=pltpu.CompilerParams(vmem_limit_bytes=VMEM_LIMIT),
        cost_estimate=pl.CostEstimate(flops=flops, bytes_accessed=1 << 21, transcendentals=0),
    )(*args)


def product_kernel(planes, partner, plane_ref, left_ref, *refs):
    chunks, outs, total = refs[: -planes - 1], refs[-planes - 1 : -1], refs[-1]
    plane = plane_ref[0]
    rows = LANES // planes
    left = left_ref[...]
    for c in range(0, len(chunks), 2):
        right = jnp.concatenate([chunks[c][...], chunks[c + 1][...]], axis=1)
        total[:, c * LANES : (c + 2) * LANES] = dot(left, right)
    for k, out in enumerate(outs):
        for mat in range(2):
            at = pl.ds(pl.multiple_of(mat * LANES + partner(plane, k) * rows, rows), rows)
            out[mat] = total[at, :].astype(out.dtype)


def arrange_kernel(planes, place_ref, *refs):
    chunks, out = refs[:GROUP], refs[GROUP]
    place = place_ref[0]
    nodes, width = out.shape
    rows = LANES // planes
    at = pl.ds(pl.multiple_of(place * nodes, nodes), nodes)
    source = iota((LANES, width), 0)
    target = iota((LANES, width), 1)
    total = jnp.zeros((nodes, width), F32)
    for k, chunk in enumerate(chunks):
        wanted = (source // rows) * (GROUP * rows) + (place ^ k) * rows + source % rows
        total = total + dot(chunk[at, :], (wanted == target).astype(F32).astype(BF16))
    out[...] = total.astype(BF16)


def place_kernel(planes, bands, factor, place_ref, band_ref, *refs):
    parts, outs = refs[:planes], refs[planes:]
    place, band = place_ref[0], band_ref[0]
    _, rows, width = parts[0].shape
    width = width // bands
    for mat, out in enumerate(outs):
        for j in range(bands):
            chunks = []
            for c in range(GROUP):
                at = pl.ds(pl.multiple_of(j * width + (place ^ c) * LANES, LANES), LANES)
                chunks.append(sum(part[mat, :, at].astype(F32) for part in parts) * factor)
            columns = [
                jnp.concatenate([chunk[:, z * rows : (z + 1) * rows] for chunk in chunks], axis=1)
                for z in range(planes)
            ]
            target = ((band + bands - j) % bands) * width
            out[:, pl.ds(pl.multiple_of(target, LANES), width)] = jnp.concatenate(columns, axis=1)


def shards(
    orbital_block, cell_matrices, cell_nodes, shared_nodes, inv_sqrt_mass, potential, filter_center, filter_halfwidth
):
    band_count = lax.axis_size("band")
    dom_count = lax.axis_size("dom")
    planes = dom_count // GROUP
    nodes, width = orbital_block.shape
    cells, corners, _ = cell_matrices.shape
    shared = shared_nodes.shape[1]
    rows = width // dom_count
    here = lax.axis_index("dom")
    band = lax.axis_index("band")
    plane, place = here // GROUP, here % GROUP
    place_arg = place.astype(jnp.int32).reshape(1)
    everyone = range(dom_count)

    def in_plane(block, k):
        return lax.ppermute(block, "dom", [(i, i ^ k) for i in everyone])

    def partner(index, k):
        return index ^ k if planes & (planes - 1) == 0 else (2 * planes + k - index) % planes

    def to_band(block, k):
        return lax.ppermute(block, "band", [(i, (i + k) % band_count) for i in range(band_count)])

    def line(values, row):
        height, count = values.shape
        return jnp.pad(values, ((row, 8 - row - height), (0, nodes - count)))

    ids = line(cell_nodes.T, 0) + line(shared_nodes, cells)
    small = ids.astype(F32) + line(inv_sqrt_mass[None], cells + 1) + line(potential[None], cells + 2)
    messages = call(
        functools.partial(pack_kernel, planes, corners),
        [((nodes + (cells + 1) // 2 * LANES + EXTRA, LANES), BF16)] * GROUP,
        (place_arg, orbital_block, cell_matrices, small),
        spaces="svvv",
        scratch=[pltpu.VMEM((cells, LANES, LANES), F32)],
    )
    messages = [messages[0]] + [in_plane(messages[k], k) for k in range(1, GROUP)]
    slabs = []
    for message in messages:
        slabs += call(
            functools.partial(build_kernel, nodes, cells, corners, shared),
            [
                ((nodes, nodes), F32), ((shared, shared), F32), ((nodes, 2 * shared), BF16), ((2 * shared, nodes), BF16),
            ] + [((nodes, LANES), F32)] * 3,
            (filter_center, filter_halfwidth, message, slabs[-6] if slabs else message),
            spaces="ssva",
            flops=1 << 28,
        )
    height = GROUP * nodes
    column = ((height, LANES), F32)
    trace = ((FILTER_DEG * shared + 2 * shared, LANES), BF16)
    odd_arg = (plane % 2).astype(jnp.int32).reshape(1)
    own, down, up, mass, scale, diag, start, keep, *pairs = call(
        functools.partial(first_kernel, shared),
        [
            ((GROUP, nodes, nodes), BF16), ((GROUP, 2 * shared, nodes), BF16), ((GROUP, nodes, 2 * shared), BF16),
            column, column, column, ((height, LANES), BF16), ((shared, LANES), BF16), trace, trace,
        ],
        (place_arg, odd_arg, *messages, *slabs),
        spaces="ss" + "v" * (GROUP * 8),
        scratch=[
            pltpu.VMEM((GROUP, nodes, nodes), F32), pltpu.VMEM((GROUP, shared, shared), F32),
            pltpu.VMEM((height, 2 * LANES), F32), pltpu.VMEM((height, 2 * LANES), F32),
            pltpu.VMEM((2, *trace[0]), BF16),
        ],
        flops=1 << 30,
    )

    def with_neighbour(blocks):
        firsts = [z ^ 1 for z in range(planes)]
        seconds = [(z + 1 if z % 2 else z - 1) % planes for z in range(planes)]
        routes = [[(i, to[i // GROUP] * GROUP + i % GROUP) for i in everyone] for to in (firsts, seconds)]
        return [lax.ppermute(block, "dom", route) for block, route in zip(blocks, routes)]

    heard = with_neighbour(pairs)
    mine, corner, *pairs = call(
        functools.partial(second_kernel, shared),
        [((height, LANES), BF16)] + [((shared, LANES), BF16)] * 3,
        (odd_arg, own, down, up, mass, scale, diag, start, keep, *heard),
        spaces="s" + "v" * 10,
        scratch=[pltpu.VMEM((height, LANES), F32), pltpu.VMEM((height, LANES), F32), pltpu.VMEM((2, *trace[0]), BF16)],
        flops=1 << 30,
    )
    heard = with_neighbour(pairs)
    others = [in_plane(mine, k) for k in range(1, GROUP)]
    first, others[0], *heard = lax.optimization_barrier((mine, others[0], *heard))
    (left,) = call(
        functools.partial(third_kernel, shared),
        [((2 * LANES, height), BF16)],
        (odd_arg, filter_center, filter_halfwidth, own, down, up, mass, diag, mine, corner, *heard),
        spaces="sss" + "v" * 9,
        scratch=[pltpu.VMEM((2, shared, LANES), BF16)],
        flops=1 << 28,
    )

    gathered = [mine] + others
    rights = list(gathered)
    for k in range(1, band_count):
        rights += [to_band(block, k) for block in [first] + others]
    part = (2, rows, band_count * width)
    parts = list(call(
        functools.partial(product_kernel, planes, partner),
        [(part, F32)] + [(part, BF16)] * (planes - 1),
        (plane.astype(jnp.int32).reshape(1), left, *rights),
        spaces="sv" + "v" * len(rights),
        scratch=[pltpu.VMEM((2 * LANES, band_count * width), F32)],
        flops=1 << 28,
    ))
    for k in [*range(2, planes), *range(1, min(planes, 2))]:
        route = [(i, partner(i // GROUP, k) * GROUP + i % GROUP) for i in everyone]
        parts[k] = lax.ppermute(parts[k], "dom", route)
    early = [*range(2, planes), 1][0]
    *gathered, parts[early] = lax.optimization_barrier((*gathered, parts[early]))
    (filtered,) = call(
        functools.partial(arrange_kernel, planes),
        [((nodes, width), BF16)],
        (place_arg, *gathered),
        spaces="s" + "v" * GROUP,
    )
    projected, intersection = call(
        functools.partial(place_kernel, planes, band_count, 1.0 / (nodes * dom_count)),
        [((rows, band_count * width), F32)] * 2,
        (place_arg, band.astype(jnp.int32).reshape(1), *parts),
        spaces="ss" + "v" * planes,
    )
    return filtered, intersection, projected


def solution(mesh):
    return jax.shard_map(
        shards,
        mesh=mesh,
        in_specs=(
            P("dom", "band"),
            P("dom", None, None),
            P(None, "dom"),
            P("dom", None),
            P("dom"),
            P("dom"),
            P(),
            P(),
        ),
        out_specs=(P("dom", "band"), P(("band", "dom"), None), P(("band", "dom"), None)),
        check_vma=False,
    )
```

```python
import functools

import jax
import jax.numpy as jnp
from jax import lax
from jax.experimental import pallas as pl
from jax.experimental.pallas import tpu as pltpu
from jax.sharding import PartitionSpec as P

FILTER_DEG = 4
GROUP = 4
HELD = (0, 1, 3, 2)
LANES = 128
EXTRA = 32
F32 = jnp.float32
BF16 = jnp.bfloat16
VMEM_LIMIT = 20 * 1024 * 1024


def dot(a, b):
    return jnp.dot(a, b, preferred_element_type=F32)


def dot_nt(a, b):
    return lax.dot_general(a, b, (((1,), (1,)), ((), ())), preferred_element_type=F32)


def iota(shape, dim):
    return lax.broadcasted_iota(jnp.int32, shape, dim)


def split3(x):
    high = x.astype(BF16)
    rest = x - high.astype(F32)
    middle = rest.astype(BF16)
    low = (rest - middle.astype(F32)).astype(BF16)
    return high, middle, low


def pack_kernel(planes, corners, place_ref, field_ref, cells_ref, small_ref, *refs):
    out_refs, square = refs[:GROUP], refs[GROUP]
    place = place_ref[0]
    nodes, width = field_ref.shape
    cells = cells_ref.shape[0]
    rows = LANES // planes
    line, lane = iota((LANES, LANES), 0), iota((LANES, LANES), 1)
    square[...] = jnp.zeros_like(square)
    for c in range(cells):
        square[c, 0:corners, 0:corners] = cells_ref[c].astype(F32)
    for c in range(0, cells, 2):
        first = square[c]
        second = square[c + 1] if c + 1 < cells else jnp.zeros_like(first)
        diagonal = 0.5 * jnp.sum(jnp.where(line == lane, second, 0.0), axis=0, keepdims=True)
        packed = jnp.where(line < lane, first, jnp.where(line > lane, second, 0.5 * first))
        packed = jnp.where(line == LANES - 1, diagonal, packed)
        for out in out_refs:
            out[nodes + c // 2 * LANES : nodes + (c // 2 + 1) * LANES, :] = packed.astype(BF16)
    small = small_ref[...]
    ids = small[0:cells, 0:LANES]
    high = jnp.floor(ids * (1.0 / 64.0))
    high = jnp.where(iota((cells, LANES), 1) < corners, high, -8.0)
    pieces = [high, ids - 64.0 * jnp.maximum(high, 0.0), small[cells : cells + 1, 0:LANES]]
    for j in (1, 2):
        for part in split3(small[cells + j : cells + j + 1]):
            pieces += [part[:, h * LANES : (h + 1) * LANES].astype(F32) for h in range(nodes // LANES)]
    used = sum(piece.shape[0] for piece in pieces)
    pieces.append(jnp.zeros((EXTRA - used, LANES), F32))
    for out in out_refs:
        out[nodes + (cells + 1) // 2 * LANES :, :] = jnp.concatenate(pieces, axis=0).astype(BF16)
    source = iota((width, LANES), 0)
    target = iota((width, LANES), 1)
    wanted = (target // rows) * (GROUP * rows) + target % rows
    for k in range(GROUP):
        pick = wanted + (place ^ k) * rows == source
        out_refs[k][0:nodes, :] = dot(field_ref[...], pick.astype(F32).astype(BF16)).astype(BF16)


def apply_plane(whole, up, fields, outside, keep=range(GROUP)):
    shared = up[0].shape[1] // 2
    nodes = up[0].shape[0]
    products = [dot(matrix, field) for matrix, field in zip(whole, fields)]
    to_next = [product[nodes : nodes + shared] for product in products]
    to_previous = [product[nodes + shared :] for product in products]
    nothing = jnp.zeros_like(to_next[0])
    below, above = outside(to_previous[0], to_next[GROUP - 1]) if outside else (nothing, nothing)
    sums = []
    for i in range(GROUP):
        if i not in keep:
            sums.append(None)
            continue
        sides = [above if i == GROUP - 1 else to_previous[i + 1], below if i == 0 else to_next[i - 1]]
        sums.append(products[i][:nodes] + dot(up[i], jnp.concatenate(sides, axis=0).astype(BF16)))
    return sums, to_next[GROUP - 1], to_previous[0]


def build_kernel(
    nodes, cells, corners, shared, center_ref, half_ref, ref, _, own_ref, corner_ref, up_ref, down_ref, mass_ref, scale_ref, diag_ref,
):
    center, half = center_ref[0], half_ref[0]
    both = nodes + shared
    halves = nodes // LANES
    base = nodes + (cells + 1) // 2 * LANES
    line, lane = iota((LANES, LANES), 0), iota((LANES, LANES), 1)
    nothing = jnp.zeros((LANES, LANES), F32)
    extra = ref[base : base + EXTRA, :].astype(F32)
    ids = 64.0 * extra[0:cells] + extra[cells : 2 * cells]
    row = 2 * cells + 1
    tables = [ids]
    for first in (row, row + 3 * halves):
        tables.append(sum(extra[first + j * halves : first + (j + 1) * halves] for j in range(3)))
    tables.append(jnp.zeros((LANES - cells - 2 * halves, LANES), F32))
    columns = jnp.transpose(jnp.concatenate(tables, axis=0))
    ids = ids.astype(jnp.int32)
    id_columns = columns[:, 0:cells].astype(jnp.int32)
    lefts, rights = [], []
    for c in range(cells):
        square = ref[nodes + c // 2 * LANES : nodes + (c // 2 + 1) * LANES, :].astype(F32)
        if c % 2 == 0:
            matrix = jnp.where(line <= lane, square, nothing)
        else:
            matrix = jnp.where((line > lane) & (line < corners), square, nothing)
            matrix = matrix + jnp.where(line == lane, square[LANES - 1 :], nothing)
        matrix = (matrix + jnp.transpose(matrix)).astype(BF16)
        pick = (iota((both, LANES), 0) == ids[c : c + 1]).astype(F32).astype(BF16)
        lefts.append(dot(pick, matrix).astype(BF16))
        rights.append((iota((LANES, both), 1) == id_columns[:, c : c + 1]).astype(F32).astype(BF16))
    total = dot(jnp.concatenate(lefts, axis=1), jnp.concatenate(rights, axis=0))
    own_ref[...] = total[:nodes, :nodes]
    corner_ref[...] = total[nodes:, nodes:]
    own_shared = extra[2 * cells : 2 * cells + 1, 0:shared].astype(jnp.int32)
    place_in = (iota((nodes, shared), 0) == own_shared).astype(F32)
    sides = jnp.concatenate([total[:nodes, nodes:], place_in], axis=1)
    up_ref[...] = sides.astype(BF16)
    down_ref[...] = jnp.transpose(sides).astype(BF16)
    for h in range(halves):
        at = slice(h * LANES, (h + 1) * LANES)
        mass = jnp.broadcast_to(columns[:, cells + h : cells + h + 1], (LANES, LANES))
        off = cells + halves + h
        pot = jnp.broadcast_to(columns[:, off : off + 1], (LANES, LANES))
        mass_ref[at, :] = mass
        scale_ref[at, :] = mass / half
        diag_ref[at, :] = (pot - center) / half


def first_kernel(shared, place_ref, odd_ref, *refs):
    messages, refs = refs[:GROUP], refs[GROUP:]
    slabs = [refs[7 * k : 7 * k + 7] for k in range(GROUP)]
    whole_ref, up_ref, mass_ref, scale_ref, diag_ref, start_ref = refs[7 * GROUP : 7 * GROUP + 6]
    keep_ref, pair0_ref, pair1_ref, raw, corner, cur, prev, box = refs[7 * GROUP + 6 :]
    next_ref, previous_ref = box.at[0], box.at[1]
    place = place_ref[0]
    nodes = whole_ref.shape[2]
    for k in range(GROUP):
        slab = place ^ k
        at = pl.ds(pl.multiple_of(slab * nodes, nodes), nodes)
        own_k, corner_k, up_k, down_k, mass_k, scale_k, diag_k = slabs[k]
        start_ref[at, :] = messages[k][0:nodes, :]
        raw[slab] = own_k[...]
        corner[slab] = corner_k[...]
        up_ref[slab] = up_k[...]
        whole_ref[slab, nodes:, :] = down_k[...]
        mass_ref[at, :] = mass_k[...]
        scale_ref[at, :] = scale_k[...]
        diag_ref[at, :] = diag_k[...]
    whole_ref[0, 0:nodes, :] = raw[0].astype(BF16)
    for i in range(1, GROUP):
        moved = dot(corner[i - 1].astype(BF16), whole_ref[i, nodes + shared :, :])
        moved = jnp.concatenate([jnp.zeros_like(moved), moved], axis=0).astype(BF16)
        whole_ref[i, 0:nodes, :] = (raw[i] + dot(up_ref[i], moved)).astype(BF16)

    cur[:, 0:LANES] = start_ref[...].astype(F32)
    cur[:, LANES:] = jnp.zeros((GROUP * nodes, 2 * shared), F32)
    top = (GROUP - 1) * nodes
    first = up_ref[0].astype(F32)
    last = up_ref[GROUP - 1].astype(F32)
    lane = iota((nodes, 2 * shared), 1)
    swapped = jnp.concatenate([first[:, shared:], first[:, :shared]], axis=1)
    cur[0:nodes, LANES:] = jnp.where(lane < shared, swapped * scale_ref[0:nodes, :], 0.0)
    swapped = jnp.concatenate([last[:, shared:], last[:, :shared]], axis=1)
    cur[top:, LANES:] = cur[top:, LANES:] + jnp.where(lane >= shared, swapped * scale_ref[top:, :], 0.0)
    prev[...] = jnp.zeros_like(prev)

    whole = [whole_ref[i] for i in range(GROUP)]
    up = [up_ref[i] for i in range(GROUP)]

    def wide(ref, i):
        part = ref[i * nodes : (i + 1) * nodes, :]
        return jnp.concatenate([part, part], axis=1)

    next_parts, previous_parts = [], []
    for k in range(FILTER_DEG):
        last_step = k == FILTER_DEG - 1
        if last_step:
            field0 = (mass_ref[0:nodes, :] * cur[0:nodes, 0:LANES]).astype(BF16)
            field3 = (mass_ref[top:, :] * cur[top:, 0:LANES]).astype(BF16)
            next_ref[k * shared : (k + 1) * shared, :] = dot(whole_ref[GROUP - 1, nodes:, :], field3)[:shared].astype(BF16)
            previous_ref[k * shared : (k + 1) * shared, :] = dot(whole_ref[0, nodes:, :], field0)[shared:].astype(BF16)
            break
        fields = [(wide(mass_ref, i) * cur[i * nodes : (i + 1) * nodes, :]).astype(BF16) for i in range(GROUP)]
        keep = range(GROUP) if k < FILTER_DEG - 2 else (0, GROUP - 1)
        sums, to_next, to_previous = apply_plane(whole, up, fields, None, keep)
        next_ref[k * shared : (k + 1) * shared, :] = to_next[:, 0:LANES].astype(BF16)
        previous_ref[k * shared : (k + 1) * shared, :] = to_previous[:, 0:LANES].astype(BF16)
        next_parts.append(to_next[:, LANES + shared :])
        previous_parts.append(to_previous[:, LANES : LANES + shared])
        for i in range(GROUP):
            if sums[i] is None:
                continue
            at = slice(i * nodes, (i + 1) * nodes)
            now = cur[at, :]
            image = wide(scale_ref, i) * sums[i] + wide(diag_ref, i) * now
            if k == 0:
                factor = jnp.where(iota((1, 2 * LANES), 1) < LANES, 1.0, 2.0)
                new = factor * image
            else:
                new = 2.0 * image - prev[at, :]
            prev[at, :] = now
            cur[at, :] = new
    at = FILTER_DEG * shared
    next_parts.append(corner[GROUP - 1])
    previous_parts.append(jnp.zeros((shared, shared), F32))
    for j in range(2):
        next_ref[at + j * shared : at + (j + 1) * shared, :] = jnp.concatenate(
            next_parts[2 * j : 2 * j + 2], axis=1
        ).astype(BF16)
        previous_ref[at + j * shared : at + (j + 1) * shared, :] = jnp.concatenate(
            previous_parts[2 * j : 2 * j + 2], axis=1
        ).astype(BF16)
    keep_ref[...] = next_ref[at + shared : at + 2 * shared, :]
    odd = odd_ref[0]
    pair0_ref[...] = box[odd]
    pair1_ref[...] = box[1 - odd]


def second_kernel(
    shared, odd_ref, whole_ref, up_ref, mass_ref, scale_ref, diag_ref, start_ref, keep_ref, from0_ref, from1_ref,
    filtered_ref, corner_ref, pair0_ref, pair1_ref, cur, prev, box,
):
    odd = odd_ref[0]
    box[0] = from0_ref[...]
    box[1] = from1_ref[...]
    above_ref, below_ref = box.at[odd], box.at[1 - odd]
    nodes = whole_ref.shape[2]
    whole = [whole_ref[i] for i in range(GROUP)]
    up = [up_ref[i] for i in range(GROUP)]
    at = FILTER_DEG * shared
    near_b, far_b = below_ref[at : at + shared, :], below_ref[at + shared : at + 2 * shared, :]
    near_a, far_a = above_ref[at : at + shared, :], above_ref[at + shared : at + 2 * shared, :]
    mine = keep_ref[...]
    corner_ref[...] = far_b
    zero = jnp.zeros((shared, LANES), BF16)
    below_past, above_past = [], []

    def past(items, lag):
        if lag > len(items):
            return zero
        item = items[len(items) - lag]
        return item if lag == len(items) else item * 2

    def pair(a, b):
        return jnp.concatenate([a, b], axis=0)

    for k in range(FILTER_DEG):

        def outside(to_previous, to_next, k=k):
            here = to_previous.astype(BF16)
            below = below_ref[k * shared : (k + 1) * shared, :].astype(F32)
            below = below + dot(near_b, pair(past(below_past, 1), past(below_past, 2)))
            below = below + dot(far_b, pair(past(below_past, 3), here))
            above = above_ref[k * shared : (k + 1) * shared, :].astype(F32)
            above = above + dot(near_a, pair(past(above_past, 1), past(above_past, 2)))
            above = above + dot(far_a, pair(past(above_past, 3), zero))
            force = to_next + dot(mine, pair(zero, above.astype(BF16)))
            below_past.append(here)
            above_past.append(force.astype(BF16))
            return below, above

        fields, values = [], []
        for i in range(GROUP):
            rows = slice(i * nodes, (i + 1) * nodes)
            values.append(start_ref[rows, :].astype(F32) if k == 0 else cur[rows, :])
            fields.append((mass_ref[rows, :] * values[i]).astype(BF16))
        sums, _, _ = apply_plane(whole, up, fields, outside)
        for i in range(GROUP):
            rows = slice(i * nodes, (i + 1) * nodes)
            image = scale_ref[rows, :] * sums[i] + diag_ref[rows, :] * values[i]
            new = image if k == 0 else 2.0 * image - prev[rows, :]
            if k == FILTER_DEG - 1:
                filtered_ref[rows, :] = new.astype(BF16)
            else:
                prev[rows, :] = values[i]
                cur[rows, :] = new
    top = (GROUP - 1) * nodes
    field0 = (mass_ref[0:nodes, :] * filtered_ref[0:nodes, :].astype(F32)).astype(BF16)
    field3 = (mass_ref[top:, :] * filtered_ref[top:, :].astype(F32)).astype(BF16)
    box[0, 0:shared, :] = dot(whole_ref[GROUP - 1, nodes:, :], field3)[:shared].astype(BF16)
    box[1, 0:shared, :] = dot(whole_ref[0, nodes:, :], field0)[shared:].astype(BF16)
    pair0_ref[...] = box[odd, 0:shared, :]
    pair1_ref[...] = box[1 - odd, 0:shared, :]


def third_kernel(
    shared, odd_ref, center_ref, half_ref, whole_ref, up_ref, mass_ref, diag_ref, filtered_ref, corner_ref,
    from0_ref, from1_ref, *refs,
):
    left_ref, box = refs[-2:]
    nodes = whole_ref.shape[2]
    center, half = center_ref[0], half_ref[0]
    whole = [whole_ref[i] for i in range(GROUP)]
    up = [up_ref[i] for i in range(GROUP)]
    odd = odd_ref[0]
    box[0] = from0_ref[...]
    box[1] = from1_ref[...]
    above_ref, below_ref = box.at[odd], box.at[1 - odd]
    far_b = corner_ref[...]
    zero = jnp.zeros((shared, LANES), BF16)

    def outside(to_previous, to_next):
        below = below_ref[...].astype(F32)
        below = below + dot(far_b, jnp.concatenate([zero, to_previous.astype(BF16)], axis=0))
        return below, above_ref[...].astype(F32)

    values = [filtered_ref[i * nodes : (i + 1) * nodes, :].astype(F32) for i in range(GROUP)]
    fields = [(mass_ref[i * nodes : (i + 1) * nodes, :] * values[i]).astype(BF16) for i in range(GROUP)]
    sums, _, _ = apply_plane(whole, up, fields, outside)
    for i in range(GROUP):
        rows = slice(i * nodes, (i + 1) * nodes)
        pot = diag_ref[rows, :] * half + center
        applied = mass_ref[rows, :] * sums[i] + pot * values[i]
        left_ref[0:LANES, rows] = jnp.transpose(applied).astype(BF16)
        left_ref[LANES:, rows] = jnp.transpose(values[i]).astype(BF16)


SPACES = {"s": pltpu.SMEM, "v": pltpu.VMEM, "a": pl.ANY}


def call(kernel, outs, args, spaces=None, scratch=(), flops=0):
    spaces = spaces or "v" * len(args)
    return pl.pallas_call(
        kernel,
        out_shape=[jax.ShapeDtypeStruct(shape, dtype) for shape, dtype in outs],
        in_specs=[pl.BlockSpec(memory_space=SPACES[space]) for space in spaces],
        out_specs=[pl.BlockSpec(memory_space=pltpu.VMEM)] * len(outs),
        scratch_shapes=list(scratch),
        compiler_params=pltpu.CompilerParams(vmem_limit_bytes=VMEM_LIMIT),
        cost_estimate=pl.CostEstimate(flops=flops, bytes_accessed=1 << 21, transcendentals=0),
    )(*args)


def product_kernel(left_ref, *refs):
    chunks, out = refs[:-1], refs[-1]
    left = left_ref[...]
    for c in range(0, len(chunks), 2):
        right = jnp.concatenate([chunks[c][...], chunks[c + 1][...]], axis=1)
        out[:, c * LANES : (c + 2) * LANES] = dot(left, right).astype(out.dtype)


def cut_kernel(planes, partner, plane_ref, left_ref, half_ref, *refs):
    chunks, outs, total = refs[: -planes - 1], refs[-planes - 1 : -1], refs[-1]
    plane = plane_ref[0]
    rows = LANES // planes
    width = half_ref.shape[1]
    product_kernel(left_ref, *chunks, total)
    for k, out in enumerate(outs):
        for mat in range(2):
            at = pl.ds(pl.multiple_of(mat * LANES + partner(plane, k) * rows, rows), rows)
            out[mat, :, 0:width] = half_ref[at, :].astype(out.dtype)
            out[mat, :, width:] = total[at, :].astype(out.dtype)


def arrange_kernel(planes, place_ref, *refs):
    chunks, out = refs[:GROUP], refs[GROUP]
    place = place_ref[0]
    nodes, width = out.shape
    rows = LANES // planes
    at = pl.ds(pl.multiple_of(place * nodes, nodes), nodes)
    source = iota((LANES, width), 0)
    target = iota((LANES, width), 1)
    total = jnp.zeros((nodes, width), F32)
    for k, chunk in enumerate(chunks):
        wanted = (source // rows) * (GROUP * rows) + (place ^ HELD[k]) * rows + source % rows
        total = total + dot(chunk[at, :], (wanted == target).astype(F32).astype(BF16))
    out[...] = total.astype(BF16)


def place_kernel(planes, bands, factor, place_ref, band_ref, *refs):
    parts, outs = refs[:planes], refs[planes:]
    place, band = place_ref[0], band_ref[0]
    _, rows, width = parts[0].shape
    width = width // bands
    for mat, out in enumerate(outs):
        for j in range(bands):
            chunks = []
            for c in range(GROUP):
                slot = place ^ c
                slot = jnp.where(slot > 1, 5 - slot, slot)
                at = pl.ds(pl.multiple_of(j * width + slot * LANES, LANES), LANES)
                chunks.append(sum(part[mat, :, at].astype(F32) for part in parts) * factor)
            columns = [
                jnp.concatenate([chunk[:, z * rows : (z + 1) * rows] for chunk in chunks], axis=1)
                for z in range(planes)
            ]
            target = ((band + bands - j) % bands) * width
            out[:, pl.ds(pl.multiple_of(target, LANES), width)] = jnp.concatenate(columns, axis=1)


def shards(
    orbital_block, cell_matrices, cell_nodes, shared_nodes, inv_sqrt_mass, potential, filter_center, filter_halfwidth
):
    band_count = lax.axis_size("band")
    dom_count = lax.axis_size("dom")
    planes = dom_count // GROUP
    nodes, width = orbital_block.shape
    cells, corners, _ = cell_matrices.shape
    shared = shared_nodes.shape[1]
    rows = width // dom_count
    here = lax.axis_index("dom")
    band = lax.axis_index("band")
    plane, place = here // GROUP, here % GROUP
    place_arg = place.astype(jnp.int32).reshape(1)
    everyone = range(dom_count)

    def in_plane(block, k):
        return lax.ppermute(block, "dom", [(i, i ^ k) for i in everyone])

    def partner(index, k):
        return index ^ k if planes & (planes - 1) == 0 else (2 * planes + k - index) % planes

    def to_band(block, k):
        return lax.ppermute(block, "band", [(i, (i + k) % band_count) for i in range(band_count)])

    def line(values, row):
        height, count = values.shape
        return jnp.pad(values, ((row, 8 - row - height), (0, nodes - count)))

    ids = line(cell_nodes.T, 0) + line(shared_nodes, cells)
    small = ids.astype(F32) + line(inv_sqrt_mass[None], cells + 1) + line(potential[None], cells + 2)
    messages = call(
        functools.partial(pack_kernel, planes, corners),
        [((nodes + (cells + 1) // 2 * LANES + EXTRA, LANES), BF16)] * GROUP,
        (place_arg, orbital_block, cell_matrices, small),
        spaces="svvv",
        scratch=[pltpu.VMEM((cells, LANES, LANES), F32)],
    )
    messages = [messages[0]] + [in_plane(messages[k], k) for k in range(1, GROUP)]
    slabs = []
    for message in messages:
        slabs += call(
            functools.partial(build_kernel, nodes, cells, corners, shared),
            [
                ((nodes, nodes), F32), ((shared, shared), F32), ((nodes, 2 * shared), BF16), ((2 * shared, nodes), BF16),
            ] + [((nodes, LANES), F32)] * 3,
            (filter_center, filter_halfwidth, message, slabs[-6] if slabs else message),
            spaces="ssva",
            flops=1 << 28,
        )
    height = GROUP * nodes
    column = ((height, LANES), F32)
    trace = ((FILTER_DEG * shared + 2 * shared, LANES), BF16)
    odd_arg = (plane % 2).astype(jnp.int32).reshape(1)
    whole, up, mass, scale, diag, start, keep, *pairs = call(
        functools.partial(first_kernel, shared),
        [
            ((GROUP, nodes + 2 * shared, nodes), BF16), ((GROUP, nodes, 2 * shared), BF16),
            column, column, column, ((height, LANES), BF16), ((shared, LANES), BF16), trace, trace,
        ],
        (place_arg, odd_arg, *messages, *slabs),
        spaces="ss" + "v" * (GROUP * 8),
        scratch=[
            pltpu.VMEM((GROUP, nodes, nodes), F32), pltpu.VMEM((GROUP, shared, shared), F32),
            pltpu.VMEM((height, 2 * LANES), F32), pltpu.VMEM((height, 2 * LANES), F32),
            pltpu.VMEM((2, *trace[0]), BF16),
        ],
        flops=1 << 30,
    )

    def with_neighbour(blocks):
        firsts = [z ^ 1 for z in range(planes)]
        seconds = [(z + 1 if z % 2 else z - 1) % planes for z in range(planes)]
        routes = [[(i, to[i // GROUP] * GROUP + i % GROUP) for i in everyone] for to in (firsts, seconds)]
        return [lax.ppermute(block, "dom", route) for block, route in zip(blocks, routes)]

    heard = with_neighbour(pairs)
    mine, corner, *pairs = call(
        functools.partial(second_kernel, shared),
        [((height, LANES), BF16)] + [((shared, LANES), BF16)] * 3,
        (odd_arg, whole, up, mass, scale, diag, start, keep, *heard),
        spaces="s" + "v" * 9,
        scratch=[pltpu.VMEM((height, LANES), F32), pltpu.VMEM((height, LANES), F32), pltpu.VMEM((2, *trace[0]), BF16)],
        flops=1 << 30,
    )
    heard = with_neighbour(pairs)
    others = [in_plane(mine, k) for k in HELD[1:]]
    first, others[0], *heard = lax.optimization_barrier((mine, others[0], *heard))
    swapped = [[to_band(block, k) for block in (first, others[0])] for k in range(1, band_count)]
    (left,) = call(
        functools.partial(third_kernel, shared),
        [((2 * LANES, height), BF16)],
        (odd_arg, filter_center, filter_halfwidth, whole, up, mass, diag, mine, corner, *heard, *sum(swapped, [])),
        spaces="sss" + "v" * 8 + "a" * 2 * (band_count - 1),
        scratch=[pltpu.VMEM((2, shared, LANES), BF16)],
        flops=1 << 28,
    )

    gathered = [mine] + others
    rights = list(gathered)
    for k in range(1, band_count):
        rights += swapped[k - 1] + [to_band(block, k) for block in others[1:]]
    part = (2, rows, band_count * width)
    (half,) = call(product_kernel, [((2 * LANES, width), F32)], (left, *rights[:GROUP]), flops=1 << 28)
    parts = list(call(
        functools.partial(cut_kernel, planes, partner),
        [(part, F32)] + [(part, BF16)] * (planes - 1),
        (plane.astype(jnp.int32).reshape(1), left, half, *rights[GROUP:]),
        spaces="svv" + "v" * (len(rights) - GROUP),
        scratch=[pltpu.VMEM((2 * LANES, (band_count - 1) * width), F32)],
        flops=1 << 28,
    ))
    for k in [*range(2, planes), *range(1, min(planes, 2))]:
        route = [(i, partner(i // GROUP, k) * GROUP + i % GROUP) for i in everyone]
        parts[k] = lax.ppermute(parts[k], "dom", route)
    early = [*range(2, planes), 1][0]
    *gathered, parts[early] = lax.optimization_barrier((*gathered, parts[early]))
    (filtered,) = call(
        functools.partial(arrange_kernel, planes),
        [((nodes, width), BF16)],
        (place_arg, *gathered),
        spaces="s" + "v" * GROUP,
    )
    projected, intersection = call(
        functools.partial(place_kernel, planes, band_count, 1.0 / (nodes * dom_count)),
        [((rows, band_count * width), F32)] * 2,
        (place_arg, band.astype(jnp.int32).reshape(1), *parts),
        spaces="ss" + "v" * planes,
    )
    return filtered, intersection, projected


def solution(mesh):
    return jax.shard_map(
        shards,
        mesh=mesh,
        in_specs=(
            P("dom", "band"),
            P("dom", None, None),
            P(None, "dom"),
            P("dom", None),
            P("dom"),
            P("dom"),
            P(),
            P(),
        ),
        out_specs=(P("dom", "band"), P(("band", "dom"), None), P(("band", "dom"), None)),
        check_vma=False,
    )
```

```python
import functools

import jax
import jax.numpy as jnp
from jax import lax
from jax.experimental import pallas as pl
from jax.experimental.pallas import tpu as pltpu
from jax.sharding import PartitionSpec as P

FILTER_DEG = 4
GROUP = 4
HELD = (0, 3, 2, 1)
LANES = 128
EXTRA = 32
F32 = jnp.float32
BF16 = jnp.bfloat16
VMEM_LIMIT = 20 * 1024 * 1024


def dot(a, b):
    return jnp.dot(a, b, preferred_element_type=F32)


def dot_nt(a, b):
    return lax.dot_general(a, b, (((1,), (1,)), ((), ())), preferred_element_type=F32)


def iota(shape, dim):
    return lax.broadcasted_iota(jnp.int32, shape, dim)


def split3(x):
    high = x.astype(BF16)
    rest = x - high.astype(F32)
    middle = rest.astype(BF16)
    low = (rest - middle.astype(F32)).astype(BF16)
    return high, middle, low


def pack_kernel(planes, corners, place_ref, field_ref, cells_ref, small_ref, *refs):
    out_refs, square = refs[:GROUP], refs[GROUP]
    place = place_ref[0]
    nodes, width = field_ref.shape
    cells = cells_ref.shape[0]
    rows = LANES // planes
    line, lane = iota((LANES, LANES), 0), iota((LANES, LANES), 1)
    square[...] = jnp.zeros_like(square)
    for c in range(cells):
        square[c, 0:corners, 0:corners] = cells_ref[c].astype(F32)
    for c in range(0, cells, 2):
        first = square[c]
        second = square[c + 1] if c + 1 < cells else jnp.zeros_like(first)
        diagonal = 0.5 * jnp.sum(jnp.where(line == lane, second, 0.0), axis=0, keepdims=True)
        packed = jnp.where(line < lane, first, jnp.where(line > lane, second, 0.5 * first))
        packed = jnp.where(line == LANES - 1, diagonal, packed)
        for out in out_refs:
            out[nodes + c // 2 * LANES : nodes + (c // 2 + 1) * LANES, :] = packed.astype(BF16)
    small = small_ref[...]
    ids = small[0:cells, 0:LANES]
    high = jnp.floor(ids * (1.0 / 64.0))
    high = jnp.where(iota((cells, LANES), 1) < corners, high, -8.0)
    pieces = [high, ids - 64.0 * jnp.maximum(high, 0.0), small[cells : cells + 1, 0:LANES]]
    for j in (1, 2):
        for part in split3(small[cells + j : cells + j + 1]):
            pieces += [part[:, h * LANES : (h + 1) * LANES].astype(F32) for h in range(nodes // LANES)]
    used = sum(piece.shape[0] for piece in pieces)
    pieces.append(jnp.zeros((EXTRA - used, LANES), F32))
    for out in out_refs:
        out[nodes + (cells + 1) // 2 * LANES :, :] = jnp.concatenate(pieces, axis=0).astype(BF16)
    source = iota((width, LANES), 0)
    target = iota((width, LANES), 1)
    wanted = (target // rows) * (GROUP * rows) + target % rows
    for k in range(GROUP):
        pick = wanted + (place ^ k) * rows == source
        out_refs[k][0:nodes, :] = dot(field_ref[...], pick.astype(F32).astype(BF16)).astype(BF16)


def apply_plane(whole, up, fields, outside, keep=range(GROUP)):
    shared = up[0].shape[1] // 2
    nodes = up[0].shape[0]
    products = [dot(matrix, field) for matrix, field in zip(whole, fields)]
    to_next = [product[nodes : nodes + shared] for product in products]
    to_previous = [product[nodes + shared :] for product in products]
    nothing = jnp.zeros_like(to_next[0])
    below, above = outside(to_previous[0], to_next[GROUP - 1]) if outside else (nothing, nothing)
    sums = []
    for i in range(GROUP):
        if i not in keep:
            sums.append(None)
            continue
        sides = [above if i == GROUP - 1 else to_previous[i + 1], below if i == 0 else to_next[i - 1]]
        sums.append(products[i][:nodes] + dot(up[i], jnp.concatenate(sides, axis=0).astype(BF16)))
    return sums, to_next[GROUP - 1], to_previous[0]


def build_kernel(
    nodes, cells, corners, shared, center_ref, half_ref, ref, _, own_ref, corner_ref, up_ref, down_ref, mass_ref, scale_ref, diag_ref,
):
    center, half = center_ref[0], half_ref[0]
    both = nodes + shared
    halves = nodes // LANES
    base = nodes + (cells + 1) // 2 * LANES
    line, lane = iota((LANES, LANES), 0), iota((LANES, LANES), 1)
    nothing = jnp.zeros((LANES, LANES), F32)
    extra = ref[base : base + EXTRA, :].astype(F32)
    ids = 64.0 * extra[0:cells] + extra[cells : 2 * cells]
    row = 2 * cells + 1
    tables = [ids]
    for first in (row, row + 3 * halves):
        tables.append(sum(extra[first + j * halves : first + (j + 1) * halves] for j in range(3)))
    tables.append(jnp.zeros((LANES - cells - 2 * halves, LANES), F32))
    columns = jnp.transpose(jnp.concatenate(tables, axis=0))
    ids = ids.astype(jnp.int32)
    id_columns = columns[:, 0:cells].astype(jnp.int32)
    lefts, rights = [], []
    for c in range(cells):
        square = ref[nodes + c // 2 * LANES : nodes + (c // 2 + 1) * LANES, :].astype(F32)
        if c % 2 == 0:
            matrix = jnp.where(line <= lane, square, nothing)
        else:
            matrix = jnp.where((line > lane) & (line < corners), square, nothing)
            matrix = matrix + jnp.where(line == lane, square[LANES - 1 :], nothing)
        matrix = (matrix + jnp.transpose(matrix)).astype(BF16)
        pick = (iota((both, LANES), 0) == ids[c : c + 1]).astype(F32).astype(BF16)
        lefts.append(dot(pick, matrix).astype(BF16))
        rights.append((iota((LANES, both), 1) == id_columns[:, c : c + 1]).astype(F32).astype(BF16))
    total = dot(jnp.concatenate(lefts, axis=1), jnp.concatenate(rights, axis=0))
    own_ref[...] = total[:nodes, :nodes]
    corner_ref[...] = total[nodes:, nodes:]
    own_shared = extra[2 * cells : 2 * cells + 1, 0:shared].astype(jnp.int32)
    place_in = (iota((nodes, shared), 0) == own_shared).astype(F32)
    sides = jnp.concatenate([total[:nodes, nodes:], place_in], axis=1)
    up_ref[...] = sides.astype(BF16)
    down_ref[...] = jnp.transpose(sides).astype(BF16)
    for h in range(halves):
        at = slice(h * LANES, (h + 1) * LANES)
        mass = jnp.broadcast_to(columns[:, cells + h : cells + h + 1], (LANES, LANES))
        off = cells + halves + h
        pot = jnp.broadcast_to(columns[:, off : off + 1], (LANES, LANES))
        mass_ref[at, :] = mass
        scale_ref[at, :] = mass / half
        diag_ref[at, :] = (pot - center) / half


def first_kernel(shared, place_ref, odd_ref, *refs):
    messages, refs = refs[:GROUP], refs[GROUP:]
    slabs = [refs[7 * k : 7 * k + 7] for k in range(GROUP)]
    whole_ref, up_ref, mass_ref, scale_ref, diag_ref, start_ref = refs[7 * GROUP : 7 * GROUP + 6]
    keep_ref, pair0_ref, pair1_ref, raw, corner, cur, prev, box = refs[7 * GROUP + 6 :]
    next_ref, previous_ref = box.at[0], box.at[1]
    place = place_ref[0]
    nodes = whole_ref.shape[2]
    for k in range(GROUP):
        slab = place ^ k
        at = pl.ds(pl.multiple_of(slab * nodes, nodes), nodes)
        own_k, corner_k, up_k, down_k, mass_k, scale_k, diag_k = slabs[k]
        start_ref[at, :] = messages[k][0:nodes, :]
        raw[slab] = own_k[...]
        corner[slab] = corner_k[...]
        up_ref[slab] = up_k[...]
        whole_ref[slab, nodes:, :] = down_k[...]
        mass_ref[at, :] = mass_k[...]
        scale_ref[at, :] = scale_k[...]
        diag_ref[at, :] = diag_k[...]
    whole_ref[0, 0:nodes, :] = raw[0].astype(BF16)
    for i in range(1, GROUP):
        moved = dot(corner[i - 1].astype(BF16), whole_ref[i, nodes + shared :, :])
        moved = jnp.concatenate([jnp.zeros_like(moved), moved], axis=0).astype(BF16)
        whole_ref[i, 0:nodes, :] = (raw[i] + dot(up_ref[i], moved)).astype(BF16)

    cur[:, 0:LANES] = start_ref[...].astype(F32)
    cur[:, LANES:] = jnp.zeros((GROUP * nodes, 2 * shared), F32)
    top = (GROUP - 1) * nodes
    first = up_ref[0].astype(F32)
    last = up_ref[GROUP - 1].astype(F32)
    lane = iota((nodes, 2 * shared), 1)
    swapped = jnp.concatenate([first[:, shared:], first[:, :shared]], axis=1)
    cur[0:nodes, LANES:] = jnp.where(lane < shared, swapped * scale_ref[0:nodes, :], 0.0)
    swapped = jnp.concatenate([last[:, shared:], last[:, :shared]], axis=1)
    cur[top:, LANES:] = cur[top:, LANES:] + jnp.where(lane >= shared, swapped * scale_ref[top:, :], 0.0)
    prev[...] = jnp.zeros_like(prev)

    whole = [whole_ref[i] for i in range(GROUP)]
    up = [up_ref[i] for i in range(GROUP)]

    def wide(ref, i):
        part = ref[i * nodes : (i + 1) * nodes, :]
        return jnp.concatenate([part, part], axis=1)

    next_parts, previous_parts = [], []
    for k in range(FILTER_DEG):
        last_step = k == FILTER_DEG - 1
        if last_step:
            field0 = (mass_ref[0:nodes, :] * cur[0:nodes, 0:LANES]).astype(BF16)
            field3 = (mass_ref[top:, :] * cur[top:, 0:LANES]).astype(BF16)
            next_ref[k * shared : (k + 1) * shared, :] = dot(whole_ref[GROUP - 1, nodes:, :], field3)[:shared].astype(BF16)
            previous_ref[k * shared : (k + 1) * shared, :] = dot(whole_ref[0, nodes:, :], field0)[shared:].astype(BF16)
            break
        fields = [(wide(mass_ref, i) * cur[i * nodes : (i + 1) * nodes, :]).astype(BF16) for i in range(GROUP)]
        keep = range(GROUP) if k < FILTER_DEG - 2 else (0, GROUP - 1)
        sums, to_next, to_previous = apply_plane(whole, up, fields, None, keep)
        next_ref[k * shared : (k + 1) * shared, :] = to_next[:, 0:LANES].astype(BF16)
        previous_ref[k * shared : (k + 1) * shared, :] = to_previous[:, 0:LANES].astype(BF16)
        next_parts.append(to_next[:, LANES + shared :])
        previous_parts.append(to_previous[:, LANES : LANES + shared])
        for i in range(GROUP):
            if sums[i] is None:
                continue
            at = slice(i * nodes, (i + 1) * nodes)
            now = cur[at, :]
            image = wide(scale_ref, i) * sums[i] + wide(diag_ref, i) * now
            if k == 0:
                factor = jnp.where(iota((1, 2 * LANES), 1) < LANES, 1.0, 2.0)
                new = factor * image
            else:
                new = 2.0 * image - prev[at, :]
            prev[at, :] = now
            cur[at, :] = new
    at = FILTER_DEG * shared
    next_parts.append(corner[GROUP - 1])
    previous_parts.append(jnp.zeros((shared, shared), F32))
    for j in range(2):
        next_ref[at + j * shared : at + (j + 1) * shared, :] = jnp.concatenate(
            next_parts[2 * j : 2 * j + 2], axis=1
        ).astype(BF16)
        previous_ref[at + j * shared : at + (j + 1) * shared, :] = jnp.concatenate(
            previous_parts[2 * j : 2 * j + 2], axis=1
        ).astype(BF16)
    keep_ref[...] = next_ref[at + shared : at + 2 * shared, :]
    odd = odd_ref[0]
    pair0_ref[...] = box[odd]
    pair1_ref[...] = box[1 - odd]


def second_kernel(
    shared, odd_ref, whole_ref, up_ref, mass_ref, scale_ref, diag_ref, start_ref, keep_ref, from0_ref, from1_ref,
    filtered_ref, corner_ref, pair0_ref, pair1_ref, cur, prev, box,
):
    odd = odd_ref[0]
    box[0] = from0_ref[...]
    box[1] = from1_ref[...]
    above_ref, below_ref = box.at[odd], box.at[1 - odd]
    nodes = whole_ref.shape[2]
    whole = [whole_ref[i] for i in range(GROUP)]
    up = [up_ref[i] for i in range(GROUP)]
    at = FILTER_DEG * shared
    near_b, far_b = below_ref[at : at + shared, :], below_ref[at + shared : at + 2 * shared, :]
    near_a, far_a = above_ref[at : at + shared, :], above_ref[at + shared : at + 2 * shared, :]
    mine = keep_ref[...]
    corner_ref[...] = far_b
    zero = jnp.zeros((shared, LANES), BF16)
    below_past, above_past = [], []

    def past(items, lag):
        if lag > len(items):
            return zero
        item = items[len(items) - lag]
        return item if lag == len(items) else item * 2

    def pair(a, b):
        return jnp.concatenate([a, b], axis=0)

    for k in range(FILTER_DEG):

        def outside(to_previous, to_next, k=k):
            here = to_previous.astype(BF16)
            below = below_ref[k * shared : (k + 1) * shared, :].astype(F32)
            below = below + dot(near_b, pair(past(below_past, 1), past(below_past, 2)))
            below = below + dot(far_b, pair(past(below_past, 3), here))
            above = above_ref[k * shared : (k + 1) * shared, :].astype(F32)
            above = above + dot(near_a, pair(past(above_past, 1), past(above_past, 2)))
            above = above + dot(far_a, pair(past(above_past, 3), zero))
            force = to_next + dot(mine, pair(zero, above.astype(BF16)))
            below_past.append(here)
            above_past.append(force.astype(BF16))
            return below, above

        fields, values = [], []
        for i in range(GROUP):
            rows = slice(i * nodes, (i + 1) * nodes)
            values.append(start_ref[rows, :].astype(F32) if k == 0 else cur[rows, :])
            fields.append((mass_ref[rows, :] * values[i]).astype(BF16))
        sums, _, _ = apply_plane(whole, up, fields, outside)
        for i in range(GROUP):
            rows = slice(i * nodes, (i + 1) * nodes)
            image = scale_ref[rows, :] * sums[i] + diag_ref[rows, :] * values[i]
            new = image if k == 0 else 2.0 * image - prev[rows, :]
            if k == FILTER_DEG - 1:
                filtered_ref[rows, :] = new.astype(BF16)
            else:
                prev[rows, :] = values[i]
                cur[rows, :] = new
    top = (GROUP - 1) * nodes
    field0 = (mass_ref[0:nodes, :] * filtered_ref[0:nodes, :].astype(F32)).astype(BF16)
    field3 = (mass_ref[top:, :] * filtered_ref[top:, :].astype(F32)).astype(BF16)
    box[0, 0:shared, :] = dot(whole_ref[GROUP - 1, nodes:, :], field3)[:shared].astype(BF16)
    box[1, 0:shared, :] = dot(whole_ref[0, nodes:, :], field0)[shared:].astype(BF16)
    pair0_ref[...] = box[odd, 0:shared, :]
    pair1_ref[...] = box[1 - odd, 0:shared, :]


def third_kernel(
    shared, odd_ref, center_ref, half_ref, whole_ref, up_ref, mass_ref, diag_ref, filtered_ref, corner_ref,
    from0_ref, from1_ref, *refs,
):
    left_ref, box = refs[-2:]
    nodes = whole_ref.shape[2]
    center, half = center_ref[0], half_ref[0]
    whole = [whole_ref[i] for i in range(GROUP)]
    up = [up_ref[i] for i in range(GROUP)]
    odd = odd_ref[0]
    box[0] = from0_ref[...]
    box[1] = from1_ref[...]
    above_ref, below_ref = box.at[odd], box.at[1 - odd]
    far_b = corner_ref[...]
    zero = jnp.zeros((shared, LANES), BF16)

    def outside(to_previous, to_next):
        below = below_ref[...].astype(F32)
        below = below + dot(far_b, jnp.concatenate([zero, to_previous.astype(BF16)], axis=0))
        return below, above_ref[...].astype(F32)

    values = [filtered_ref[i * nodes : (i + 1) * nodes, :].astype(F32) for i in range(GROUP)]
    fields = [(mass_ref[i * nodes : (i + 1) * nodes, :] * values[i]).astype(BF16) for i in range(GROUP)]
    sums, _, _ = apply_plane(whole, up, fields, outside)
    for i in range(GROUP):
        rows = slice(i * nodes, (i + 1) * nodes)
        pot = diag_ref[rows, :] * half + center
        applied = mass_ref[rows, :] * sums[i] + pot * values[i]
        left_ref[0:LANES, rows] = jnp.transpose(applied).astype(BF16)
        left_ref[LANES:, rows] = jnp.transpose(values[i]).astype(BF16)


SPACES = {"s": pltpu.SMEM, "v": pltpu.VMEM, "a": pl.ANY}


def call(kernel, outs, args, spaces=None, scratch=(), flops=0):
    spaces = spaces or "v" * len(args)
    return pl.pallas_call(
        kernel,
        out_shape=[jax.ShapeDtypeStruct(shape, dtype) for shape, dtype in outs],
        in_specs=[pl.BlockSpec(memory_space=SPACES[space]) for space in spaces],
        out_specs=[pl.BlockSpec(memory_space=pltpu.VMEM)] * len(outs),
        scratch_shapes=list(scratch),
        compiler_params=pltpu.CompilerParams(vmem_limit_bytes=VMEM_LIMIT),
        cost_estimate=pl.CostEstimate(flops=flops, bytes_accessed=1 << 21, transcendentals=0),
    )(*args)


def product_kernel(left_ref, *refs):
    chunks, out = refs[:-1], refs[-1]
    left = left_ref[...]
    for c in range(0, len(chunks), 2):
        right = jnp.concatenate([chunks[c][...], chunks[c + 1][...]], axis=1)
        out[:, c * LANES : (c + 2) * LANES] = dot(left, right).astype(out.dtype)


def cut_kernel(planes, partner, plane_ref, left_ref, half_ref, *refs):
    chunks, outs, total = refs[: -planes - 1], refs[-planes - 1 : -1], refs[-1]
    plane = plane_ref[0]
    rows = LANES // planes
    width = half_ref.shape[1]
    product_kernel(left_ref, *chunks, total)
    for k, out in enumerate(outs):
        for mat in range(2):
            at = pl.ds(pl.multiple_of(mat * LANES + partner(plane, k) * rows, rows), rows)
            out[mat, :, 0:width] = half_ref[at, :].astype(out.dtype)
            out[mat, :, width:] = total[at, :].astype(out.dtype)


def arrange_kernel(planes, place_ref, *refs):
    chunks, out = refs[:GROUP], refs[GROUP]
    place = place_ref[0]
    nodes, width = out.shape
    rows = LANES // planes
    at = pl.ds(pl.multiple_of(place * nodes, nodes), nodes)
    source = iota((LANES, width), 0)
    target = iota((LANES, width), 1)
    total = jnp.zeros((nodes, width), F32)
    for k, chunk in enumerate(chunks):
        wanted = (source // rows) * (GROUP * rows) + (place ^ HELD[k]) * rows + source % rows
        total = total + dot(chunk[at, :], (wanted == target).astype(F32).astype(BF16))
    out[...] = total.astype(BF16)


def place_kernel(planes, bands, factor, place_ref, band_ref, *refs):
    parts, outs = refs[:planes], refs[planes:]
    place, band = place_ref[0], band_ref[0]
    _, rows, width = parts[0].shape
    width = width // bands
    for mat, out in enumerate(outs):
        for j in range(bands):
            chunks = []
            for c in range(GROUP):
                slot = place ^ c
                slot = jnp.where(slot % 2 == 1, 4 - slot, slot)
                at = pl.ds(pl.multiple_of(j * width + slot * LANES, LANES), LANES)
                chunks.append(sum(part[mat, :, at].astype(F32) for part in parts) * factor)
            columns = [
                jnp.concatenate([chunk[:, z * rows : (z + 1) * rows] for chunk in chunks], axis=1)
                for z in range(planes)
            ]
            target = ((band + bands - j) % bands) * width
            out[:, pl.ds(pl.multiple_of(target, LANES), width)] = jnp.concatenate(columns, axis=1)


def shards(
    orbital_block, cell_matrices, cell_nodes, shared_nodes, inv_sqrt_mass, potential, filter_center, filter_halfwidth
):
    band_count = lax.axis_size("band")
    dom_count = lax.axis_size("dom")
    planes = dom_count // GROUP
    nodes, width = orbital_block.shape
    cells, corners, _ = cell_matrices.shape
    shared = shared_nodes.shape[1]
    rows = width // dom_count
    here = lax.axis_index("dom")
    band = lax.axis_index("band")
    plane, place = here // GROUP, here % GROUP
    place_arg = place.astype(jnp.int32).reshape(1)
    everyone = range(dom_count)

    def in_plane(block, k):
        return lax.ppermute(block, "dom", [(i, i ^ k) for i in everyone])

    def partner(index, k):
        return index ^ k if planes & (planes - 1) == 0 else (2 * planes + k - index) % planes

    def to_band(block, k):
        return lax.ppermute(block, "band", [(i, (i + k) % band_count) for i in range(band_count)])

    def line(values, row):
        height, count = values.shape
        return jnp.pad(values, ((row, 8 - row - height), (0, nodes - count)))

    ids = line(cell_nodes.T, 0) + line(shared_nodes, cells)
    small = ids.astype(F32) + line(inv_sqrt_mass[None], cells + 1) + line(potential[None], cells + 2)
    messages = call(
        functools.partial(pack_kernel, planes, corners),
        [((nodes + (cells + 1) // 2 * LANES + EXTRA, LANES), BF16)] * GROUP,
        (place_arg, orbital_block, cell_matrices, small),
        spaces="svvv",
        scratch=[pltpu.VMEM((cells, LANES, LANES), F32)],
    )
    messages = [messages[0]] + [in_plane(messages[k], k) for k in range(1, GROUP)]
    slabs = []
    for message in messages:
        slabs += call(
            functools.partial(build_kernel, nodes, cells, corners, shared),
            [
                ((nodes, nodes), F32), ((shared, shared), F32), ((nodes, 2 * shared), BF16), ((2 * shared, nodes), BF16),
            ] + [((nodes, LANES), F32)] * 3,
            (filter_center, filter_halfwidth, message, slabs[-6] if slabs else message),
            spaces="ssva",
            flops=1 << 28,
        )
    height = GROUP * nodes
    column = ((height, LANES), F32)
    trace = ((FILTER_DEG * shared + 2 * shared, LANES), BF16)
    odd_arg = (plane % 2).astype(jnp.int32).reshape(1)
    whole, up, mass, scale, diag, start, keep, *pairs = call(
        functools.partial(first_kernel, shared),
        [
            ((GROUP, nodes + 2 * shared, nodes), BF16), ((GROUP, nodes, 2 * shared), BF16),
            column, column, column, ((height, LANES), BF16), ((shared, LANES), BF16), trace, trace,
        ],
        (place_arg, odd_arg, *messages, *slabs),
        spaces="ss" + "v" * (GROUP * 8),
        scratch=[
            pltpu.VMEM((GROUP, nodes, nodes), F32), pltpu.VMEM((GROUP, shared, shared), F32),
            pltpu.VMEM((height, 2 * LANES), F32), pltpu.VMEM((height, 2 * LANES), F32),
            pltpu.VMEM((2, *trace[0]), BF16),
        ],
        flops=1 << 30,
    )

    def with_neighbour(blocks):
        firsts = [z ^ 1 for z in range(planes)]
        seconds = [(z + 1 if z % 2 else z - 1) % planes for z in range(planes)]
        routes = [[(i, to[i // GROUP] * GROUP + i % GROUP) for i in everyone] for to in (firsts, seconds)]
        return [lax.ppermute(block, "dom", route) for block, route in zip(blocks, routes)]

    heard = with_neighbour(pairs)
    mine, corner, *pairs = call(
        functools.partial(second_kernel, shared),
        [((height, LANES), BF16)] + [((shared, LANES), BF16)] * 3,
        (odd_arg, whole, up, mass, scale, diag, start, keep, *heard),
        spaces="s" + "v" * 9,
        scratch=[pltpu.VMEM((height, LANES), F32), pltpu.VMEM((height, LANES), F32), pltpu.VMEM((2, *trace[0]), BF16)],
        flops=1 << 30,
    )
    heard = with_neighbour(pairs)
    others = [in_plane(mine, k) for k in HELD[1:]]
    first, others[0], *heard = lax.optimization_barrier((mine, others[0], *heard))
    swapped = [[to_band(block, k) for block in (first, others[0])] for k in range(1, band_count)]
    (left,) = call(
        functools.partial(third_kernel, shared),
        [((2 * LANES, height), BF16)],
        (odd_arg, filter_center, filter_halfwidth, whole, up, mass, diag, mine, corner, *heard, *sum(swapped, [])),
        spaces="sss" + "v" * 8 + "a" * 2 * (band_count - 1),
        scratch=[pltpu.VMEM((2, shared, LANES), BF16)],
        flops=1 << 28,
    )

    gathered = [mine] + others
    rights = list(gathered)
    for k in range(1, band_count):
        rights += swapped[k - 1] + [to_band(block, k) for block in others[1:]]
    part = (2, rows, band_count * width)
    (half,) = call(product_kernel, [((2 * LANES, width), F32)], (left, *rights[:GROUP]), flops=1 << 28)
    parts = list(call(
        functools.partial(cut_kernel, planes, partner),
        [(part, F32)] + [(part, BF16)] * (planes - 1),
        (plane.astype(jnp.int32).reshape(1), left, half, *rights[GROUP:]),
        spaces="svv" + "v" * (len(rights) - GROUP),
        scratch=[pltpu.VMEM((2 * LANES, (band_count - 1) * width), F32)],
        flops=1 << 28,
    ))
    for k in [*range(2, planes), *range(1, min(planes, 2))]:
        route = [(i, partner(i // GROUP, k) * GROUP + i % GROUP) for i in everyone]
        parts[k] = lax.ppermute(parts[k], "dom", route)
    early = [*range(2, planes), 1][0]
    *gathered, parts[early] = lax.optimization_barrier((*gathered, parts[early]))
    (filtered,) = call(
        functools.partial(arrange_kernel, planes),
        [((nodes, width), BF16)],
        (place_arg, *gathered),
        spaces="s" + "v" * GROUP,
    )
    projected, intersection = call(
        functools.partial(place_kernel, planes, band_count, 1.0 / (nodes * dom_count)),
        [((rows, band_count * width), F32)] * 2,
        (place_arg, band.astype(jnp.int32).reshape(1), *parts),
        spaces="ss" + "v" * planes,
    )
    return filtered, intersection, projected


def solution(mesh):
    return jax.shard_map(
        shards,
        mesh=mesh,
        in_specs=(
            P("dom", "band"),
            P("dom", None, None),
            P(None, "dom"),
            P("dom", None),
            P("dom"),
            P("dom"),
            P(),
            P(),
        ),
        out_specs=(P("dom", "band"), P(("band", "dom"), None), P(("band", "dom"), None)),
        check_vma=False,
    )
```

```python
import functools

import jax
import jax.numpy as jnp
from jax import lax
from jax.experimental import pallas as pl
from jax.experimental.pallas import tpu as pltpu
from jax.sharding import PartitionSpec as P

FILTER_DEG = 4
GROUP = 4
HELD = (0, 3, 2, 1)
LANES = 128
EXTRA = 32
F32 = jnp.float32
BF16 = jnp.bfloat16
VMEM_LIMIT = 20 * 1024 * 1024


def dot(a, b):
    return jnp.dot(a, b, preferred_element_type=F32)


def dot_nt(a, b):
    return lax.dot_general(a, b, (((1,), (1,)), ((), ())), preferred_element_type=F32)


def iota(shape, dim):
    return lax.broadcasted_iota(jnp.int32, shape, dim)


def split3(x):
    high = x.astype(BF16)
    rest = x - high.astype(F32)
    middle = rest.astype(BF16)
    low = (rest - middle.astype(F32)).astype(BF16)
    return high, middle, low


def pack_kernel(planes, corners, place_ref, field_ref, cells_ref, small_ref, *refs):
    out_refs, square = refs[:GROUP], refs[GROUP]
    place = place_ref[0]
    nodes, width = field_ref.shape
    cells = cells_ref.shape[0]
    rows = LANES // planes
    line, lane = iota((LANES, LANES), 0), iota((LANES, LANES), 1)
    square[...] = jnp.zeros_like(square)
    for c in range(cells):
        square[c, 0:corners, 0:corners] = cells_ref[c].astype(F32)
    for c in range(0, cells, 2):
        first = square[c]
        second = square[c + 1] if c + 1 < cells else jnp.zeros_like(first)
        diagonal = 0.5 * jnp.sum(jnp.where(line == lane, second, 0.0), axis=0, keepdims=True)
        packed = jnp.where(line < lane, first, jnp.where(line > lane, second, 0.5 * first))
        packed = jnp.where(line == LANES - 1, diagonal, packed)
        for out in out_refs:
            out[nodes + c // 2 * LANES : nodes + (c // 2 + 1) * LANES, :] = packed.astype(BF16)
    small = small_ref[...]
    ids = small[0:cells, 0:LANES]
    high = jnp.floor(ids * (1.0 / 64.0))
    high = jnp.where(iota((cells, LANES), 1) < corners, high, -8.0)
    pieces = [high, ids - 64.0 * jnp.maximum(high, 0.0), small[cells : cells + 1, 0:LANES]]
    for j in (1, 2):
        for part in split3(small[cells + j : cells + j + 1]):
            pieces += [part[:, h * LANES : (h + 1) * LANES].astype(F32) for h in range(nodes // LANES)]
    used = sum(piece.shape[0] for piece in pieces)
    pieces.append(jnp.zeros((EXTRA - used, LANES), F32))
    for out in out_refs:
        out[nodes + (cells + 1) // 2 * LANES :, :] = jnp.concatenate(pieces, axis=0).astype(BF16)
    source = iota((width, LANES), 0)
    target = iota((width, LANES), 1)
    wanted = (target // rows) * (GROUP * rows) + target % rows
    for k in range(GROUP):
        pick = wanted + (place ^ k) * rows == source
        out_refs[k][0:nodes, :] = dot(field_ref[...], pick.astype(F32).astype(BF16)).astype(BF16)


def apply_plane(whole, up, fields, outside, keep=range(GROUP)):
    shared = up[0].shape[1] // 2
    nodes = up[0].shape[0]
    products = [dot(matrix, field) for matrix, field in zip(whole, fields)]
    to_next = [product[nodes : nodes + shared] for product in products]
    to_previous = [product[nodes + shared :] for product in products]
    nothing = jnp.zeros_like(to_next[0])
    below, above = outside(to_previous[0], to_next[GROUP - 1]) if outside else (nothing, nothing)
    sums = []
    for i in range(GROUP):
        if i not in keep:
            sums.append(None)
            continue
        sides = [above if i == GROUP - 1 else to_previous[i + 1], below if i == 0 else to_next[i - 1]]
        sums.append(products[i][:nodes] + dot(up[i], jnp.concatenate(sides, axis=0).astype(BF16)))
    return sums, to_next[GROUP - 1], to_previous[0]


def build_kernel(
    nodes, cells, corners, shared, center_ref, half_ref, ref, _, own_ref, corner_ref, up_ref, down_ref, mass_ref, recip_ref,
    scale_ref, diag_ref,
):
    center, half = center_ref[0], half_ref[0]
    both = nodes + shared
    halves = nodes // LANES
    base = nodes + (cells + 1) // 2 * LANES
    line, lane = iota((LANES, LANES), 0), iota((LANES, LANES), 1)
    nothing = jnp.zeros((LANES, LANES), F32)
    extra = ref[base : base + EXTRA, :].astype(F32)
    ids = 64.0 * extra[0:cells] + extra[cells : 2 * cells]
    row = 2 * cells + 1
    tables = [ids]
    for first in (row, row + 3 * halves):
        tables.append(sum(extra[first + j * halves : first + (j + 1) * halves] for j in range(3)))
    tables.append(jnp.zeros((LANES - cells - 2 * halves, LANES), F32))
    columns = jnp.transpose(jnp.concatenate(tables, axis=0))
    ids = ids.astype(jnp.int32)
    id_columns = columns[:, 0:cells].astype(jnp.int32)
    lefts, rights = [], []
    for c in range(cells):
        square = ref[nodes + c // 2 * LANES : nodes + (c // 2 + 1) * LANES, :].astype(F32)
        if c % 2 == 0:
            matrix = jnp.where(line <= lane, square, nothing)
        else:
            matrix = jnp.where((line > lane) & (line < corners), square, nothing)
            matrix = matrix + jnp.where(line == lane, square[LANES - 1 :], nothing)
        matrix = (matrix + jnp.transpose(matrix)).astype(BF16)
        pick = (iota((both, LANES), 0) == ids[c : c + 1]).astype(F32).astype(BF16)
        lefts.append(dot(pick, matrix).astype(BF16))
        rights.append((iota((LANES, both), 1) == id_columns[:, c : c + 1]).astype(F32).astype(BF16))
    total = dot(jnp.concatenate(lefts, axis=1), jnp.concatenate(rights, axis=0))
    own_ref[...] = total[:nodes, :nodes]
    corner_ref[...] = total[nodes:, nodes:]
    own_shared = extra[2 * cells : 2 * cells + 1, 0:shared].astype(jnp.int32)
    place_in = (iota((nodes, shared), 0) == own_shared).astype(F32)
    sides = jnp.concatenate([total[:nodes, nodes:], place_in], axis=1)
    up_ref[...] = sides.astype(BF16)
    down_ref[...] = jnp.transpose(sides).astype(BF16)
    for h in range(halves):
        at = slice(h * LANES, (h + 1) * LANES)
        mass = jnp.broadcast_to(columns[:, cells + h : cells + h + 1], (LANES, LANES))
        off = cells + halves + h
        pot = jnp.broadcast_to(columns[:, off : off + 1], (LANES, LANES))
        mass_ref[at, :] = mass
        recip_ref[at, :] = 1.0 / mass
        scale_ref[at, :] = mass * mass / half
        diag_ref[at, :] = (pot - center) / half


def first_kernel(shared, place_ref, odd_ref, *refs):
    messages, refs = refs[:GROUP], refs[GROUP:]
    slabs = [refs[8 * k : 8 * k + 8] for k in range(GROUP)]
    whole_ref, up_ref, mass_ref, recip_ref, scale_ref, diag_ref, start_ref = refs[8 * GROUP : 8 * GROUP + 7]
    keep_ref, pair0_ref, pair1_ref, raw, corner, cur, prev, box = refs[8 * GROUP + 7 :]
    next_ref, previous_ref = box.at[0], box.at[1]
    place = place_ref[0]
    nodes = whole_ref.shape[2]
    for k in range(GROUP):
        slab = place ^ k
        at = pl.ds(pl.multiple_of(slab * nodes, nodes), nodes)
        own_k, corner_k, up_k, down_k, mass_k, recip_k, scale_k, diag_k = slabs[k]
        start_ref[at, :] = messages[k][0:nodes, :]
        raw[slab] = own_k[...]
        corner[slab] = corner_k[...]
        up_ref[slab] = up_k[...]
        whole_ref[slab, nodes:, :] = down_k[...]
        mass_ref[at, :] = mass_k[...]
        recip_ref[at, :] = recip_k[...]
        scale_ref[at, :] = scale_k[...]
        diag_ref[at, :] = diag_k[...]
    whole_ref[0, 0:nodes, :] = raw[0].astype(BF16)
    for i in range(1, GROUP):
        moved = dot(corner[i - 1].astype(BF16), whole_ref[i, nodes + shared :, :])
        moved = jnp.concatenate([jnp.zeros_like(moved), moved], axis=0).astype(BF16)
        whole_ref[i, 0:nodes, :] = (raw[i] + dot(up_ref[i], moved)).astype(BF16)

    cur[:, 0:LANES] = mass_ref[...] * start_ref[...].astype(F32)
    cur[:, LANES:] = jnp.zeros((GROUP * nodes, 2 * shared), F32)
    top = (GROUP - 1) * nodes
    first = up_ref[0].astype(F32)
    last = up_ref[GROUP - 1].astype(F32)
    lane = iota((nodes, 2 * shared), 1)
    swapped = jnp.concatenate([first[:, shared:], first[:, :shared]], axis=1)
    cur[0:nodes, LANES:] = jnp.where(lane < shared, swapped * scale_ref[0:nodes, :], 0.0)
    swapped = jnp.concatenate([last[:, shared:], last[:, :shared]], axis=1)
    cur[top:, LANES:] = cur[top:, LANES:] + jnp.where(lane >= shared, swapped * scale_ref[top:, :], 0.0)

    whole = [whole_ref[i] for i in range(GROUP)]
    up = [up_ref[i] for i in range(GROUP)]

    def wide(ref, i):
        part = ref[i * nodes : (i + 1) * nodes, :]
        return jnp.concatenate([part, part], axis=1)

    next_parts, previous_parts = [], []
    for k in range(FILTER_DEG):
        last_step = k == FILTER_DEG - 1
        if last_step:
            field0 = cur[0:nodes, 0:LANES].astype(BF16)
            field3 = cur[top:, 0:LANES].astype(BF16)
            next_ref[k * shared : (k + 1) * shared, :] = dot(whole_ref[GROUP - 1, nodes:, :], field3)[:shared].astype(BF16)
            previous_ref[k * shared : (k + 1) * shared, :] = dot(whole_ref[0, nodes:, :], field0)[shared:].astype(BF16)
            break
        fields = [cur[i * nodes : (i + 1) * nodes, :].astype(BF16) for i in range(GROUP)]
        keep = range(GROUP) if k < FILTER_DEG - 2 else (0, GROUP - 1)
        sums, to_next, to_previous = apply_plane(whole, up, fields, None, keep)
        next_ref[k * shared : (k + 1) * shared, :] = to_next[:, 0:LANES].astype(BF16)
        previous_ref[k * shared : (k + 1) * shared, :] = to_previous[:, 0:LANES].astype(BF16)
        next_parts.append(to_next[:, LANES + shared :])
        previous_parts.append(to_previous[:, LANES : LANES + shared])
        for i in range(GROUP):
            if sums[i] is None:
                continue
            at = slice(i * nodes, (i + 1) * nodes)
            now = cur[at, :]
            image = wide(scale_ref, i) * sums[i] + wide(diag_ref, i) * now
            if k == 0:
                factor = jnp.where(iota((1, 2 * LANES), 1) < LANES, 1.0, 2.0)
                new = factor * image
            else:
                new = 2.0 * image - prev[at, :]
            prev[at, :] = now
            cur[at, :] = new
    at = FILTER_DEG * shared
    next_parts.append(corner[GROUP - 1])
    previous_parts.append(jnp.zeros((shared, shared), F32))
    for j in range(2):
        next_ref[at + j * shared : at + (j + 1) * shared, :] = jnp.concatenate(
            next_parts[2 * j : 2 * j + 2], axis=1
        ).astype(BF16)
        previous_ref[at + j * shared : at + (j + 1) * shared, :] = jnp.concatenate(
            previous_parts[2 * j : 2 * j + 2], axis=1
        ).astype(BF16)
    keep_ref[...] = next_ref[at + shared : at + 2 * shared, :]
    odd = odd_ref[0]
    pair0_ref[...] = box[odd]
    pair1_ref[...] = box[1 - odd]


def second_kernel(
    shared, odd_ref, whole_ref, up_ref, mass_ref, recip_ref, scale_ref, diag_ref, start_ref, keep_ref, from0_ref, from1_ref,
    filtered_ref, corner_ref, pair0_ref, pair1_ref, cur, prev, box,
):
    odd = odd_ref[0]
    box[0] = from0_ref[...]
    box[1] = from1_ref[...]
    above_ref, below_ref = box.at[odd], box.at[1 - odd]
    nodes = whole_ref.shape[2]
    whole = [whole_ref[i] for i in range(GROUP)]
    up = [up_ref[i] for i in range(GROUP)]
    at = FILTER_DEG * shared
    near_b, far_b = below_ref[at : at + shared, :], below_ref[at + shared : at + 2 * shared, :]
    near_a, far_a = above_ref[at : at + shared, :], above_ref[at + shared : at + 2 * shared, :]
    mine = keep_ref[...]
    corner_ref[...] = far_b
    zero = jnp.zeros((shared, LANES), BF16)
    below_past, above_past = [], []

    def past(items, lag):
        if lag > len(items):
            return zero
        item = items[len(items) - lag]
        return item if lag == len(items) else item * 2

    def pair(a, b):
        return jnp.concatenate([a, b], axis=0)

    for k in range(FILTER_DEG):

        def outside(to_previous, to_next, k=k):
            here = to_previous.astype(BF16)
            below = below_ref[k * shared : (k + 1) * shared, :].astype(F32)
            below = below + dot(near_b, pair(past(below_past, 1), past(below_past, 2)))
            below = below + dot(far_b, pair(past(below_past, 3), here))
            above = above_ref[k * shared : (k + 1) * shared, :].astype(F32)
            above = above + dot(near_a, pair(past(above_past, 1), past(above_past, 2)))
            above = above + dot(far_a, pair(past(above_past, 3), zero))
            force = to_next + dot(mine, pair(zero, above.astype(BF16)))
            below_past.append(here)
            above_past.append(force.astype(BF16))
            return below, above

        fields, values = [], []
        for i in range(GROUP):
            rows = slice(i * nodes, (i + 1) * nodes)
            values.append(mass_ref[rows, :] * start_ref[rows, :].astype(F32) if k == 0 else cur[rows, :])
            fields.append(values[i].astype(BF16))
        sums, _, _ = apply_plane(whole, up, fields, outside)
        for i in range(GROUP):
            rows = slice(i * nodes, (i + 1) * nodes)
            image = scale_ref[rows, :] * sums[i] + diag_ref[rows, :] * values[i]
            new = image if k == 0 else 2.0 * image - prev[rows, :]
            if k == FILTER_DEG - 1:
                filtered_ref[rows, :] = (recip_ref[rows, :] * new).astype(BF16)
            else:
                prev[rows, :] = values[i]
                cur[rows, :] = new
    top = (GROUP - 1) * nodes
    field0 = (mass_ref[0:nodes, :] * filtered_ref[0:nodes, :].astype(F32)).astype(BF16)
    field3 = (mass_ref[top:, :] * filtered_ref[top:, :].astype(F32)).astype(BF16)
    box[0, 0:shared, :] = dot(whole_ref[GROUP - 1, nodes:, :], field3)[:shared].astype(BF16)
    box[1, 0:shared, :] = dot(whole_ref[0, nodes:, :], field0)[shared:].astype(BF16)
    pair0_ref[...] = box[odd, 0:shared, :]
    pair1_ref[...] = box[1 - odd, 0:shared, :]


def third_kernel(
    shared, odd_ref, center_ref, half_ref, whole_ref, up_ref, mass_ref, diag_ref, filtered_ref, corner_ref,
    from0_ref, from1_ref, *refs,
):
    left_ref, box = refs[-2:]
    nodes = whole_ref.shape[2]
    center, half = center_ref[0], half_ref[0]
    whole = [whole_ref[i] for i in range(GROUP)]
    up = [up_ref[i] for i in range(GROUP)]
    odd = odd_ref[0]
    box[0] = from0_ref[...]
    box[1] = from1_ref[...]
    above_ref, below_ref = box.at[odd], box.at[1 - odd]
    far_b = corner_ref[...]
    zero = jnp.zeros((shared, LANES), BF16)

    def outside(to_previous, to_next):
        below = below_ref[...].astype(F32)
        below = below + dot(far_b, jnp.concatenate([zero, to_previous.astype(BF16)], axis=0))
        return below, above_ref[...].astype(F32)

    values = [filtered_ref[i * nodes : (i + 1) * nodes, :].astype(F32) for i in range(GROUP)]
    fields = [(mass_ref[i * nodes : (i + 1) * nodes, :] * values[i]).astype(BF16) for i in range(GROUP)]
    sums, _, _ = apply_plane(whole, up, fields, outside)
    for i in range(GROUP):
        rows = slice(i * nodes, (i + 1) * nodes)
        pot = diag_ref[rows, :] * half + center
        applied = mass_ref[rows, :] * sums[i] + pot * values[i]
        left_ref[0:LANES, rows] = jnp.transpose(applied).astype(BF16)
        left_ref[LANES:, rows] = jnp.transpose(values[i]).astype(BF16)


SPACES = {"s": pltpu.SMEM, "v": pltpu.VMEM, "a": pl.ANY}


def call(kernel, outs, args, spaces=None, scratch=(), flops=0):
    spaces = spaces or "v" * len(args)
    return pl.pallas_call(
        kernel,
        out_shape=[jax.ShapeDtypeStruct(shape, dtype) for shape, dtype in outs],
        in_specs=[pl.BlockSpec(memory_space=SPACES[space]) for space in spaces],
        out_specs=[pl.BlockSpec(memory_space=pltpu.VMEM)] * len(outs),
        scratch_shapes=list(scratch),
        compiler_params=pltpu.CompilerParams(vmem_limit_bytes=VMEM_LIMIT),
        cost_estimate=pl.CostEstimate(flops=flops, bytes_accessed=1 << 21, transcendentals=0),
    )(*args)


def product_kernel(left_ref, *refs):
    chunks, out = refs[:-1], refs[-1]
    left = left_ref[...]
    for c in range(0, len(chunks), 2):
        right = jnp.concatenate([chunks[c][...], chunks[c + 1][...]], axis=1)
        out[:, c * LANES : (c + 2) * LANES] = dot(left, right).astype(out.dtype)


def cut_kernel(planes, partner, plane_ref, left_ref, half_ref, *refs):
    chunks, outs, total = refs[: -planes - 1], refs[-planes - 1 : -1], refs[-1]
    plane = plane_ref[0]
    rows = LANES // planes
    width = half_ref.shape[1]
    product_kernel(left_ref, *chunks, total)
    for k, out in enumerate(outs):
        for mat in range(2):
            at = pl.ds(pl.multiple_of(mat * LANES + partner(plane, k) * rows, rows), rows)
            out[mat, :, 0:width] = half_ref[at, :].astype(out.dtype)
            out[mat, :, width:] = total[at, :].astype(out.dtype)


def arrange_kernel(planes, place_ref, *refs):
    chunks, out = refs[:GROUP], refs[GROUP]
    place = place_ref[0]
    nodes, width = out.shape
    rows = LANES // planes
    at = pl.ds(pl.multiple_of(place * nodes, nodes), nodes)
    source = iota((LANES, width), 0)
    target = iota((LANES, width), 1)
    total = jnp.zeros((nodes, width), F32)
    for k, chunk in enumerate(chunks):
        wanted = (source // rows) * (GROUP * rows) + (place ^ HELD[k]) * rows + source % rows
        total = total + dot(chunk[at, :], (wanted == target).astype(F32).astype(BF16))
    out[...] = total.astype(BF16)


def place_kernel(planes, bands, factor, place_ref, band_ref, *refs):
    parts, outs = refs[:planes], refs[planes:]
    place, band = place_ref[0], band_ref[0]
    _, rows, width = parts[0].shape
    width = width // bands
    for mat, out in enumerate(outs):
        for j in range(bands):
            chunks = []
            for c in range(GROUP):
                slot = place ^ c
                slot = jnp.where(slot % 2 == 1, 4 - slot, slot)
                at = pl.ds(pl.multiple_of(j * width + slot * LANES, LANES), LANES)
                chunks.append(sum(part[mat, :, at].astype(F32) for part in parts) * factor)
            columns = [
                jnp.concatenate([chunk[:, z * rows : (z + 1) * rows] for chunk in chunks], axis=1)
                for z in range(planes)
            ]
            target = ((band + bands - j) % bands) * width
            out[:, pl.ds(pl.multiple_of(target, LANES), width)] = jnp.concatenate(columns, axis=1)


def shards(
    orbital_block, cell_matrices, cell_nodes, shared_nodes, inv_sqrt_mass, potential, filter_center, filter_halfwidth
):
    band_count = lax.axis_size("band")
    dom_count = lax.axis_size("dom")
    planes = dom_count // GROUP
    nodes, width = orbital_block.shape
    cells, corners, _ = cell_matrices.shape
    shared = shared_nodes.shape[1]
    rows = width // dom_count
    here = lax.axis_index("dom")
    band = lax.axis_index("band")
    plane, place = here // GROUP, here % GROUP
    place_arg = place.astype(jnp.int32).reshape(1)
    everyone = range(dom_count)

    def in_plane(block, k):
        return lax.ppermute(block, "dom", [(i, i ^ k) for i in everyone])

    def partner(index, k):
        return index ^ k if planes & (planes - 1) == 0 else (2 * planes + k - index) % planes

    def to_band(block, k):
        return lax.ppermute(block, "band", [(i, (i + k) % band_count) for i in range(band_count)])

    def line(values, row):
        height, count = values.shape
        return jnp.pad(values, ((row, 8 - row - height), (0, nodes - count)))

    ids = line(cell_nodes.T, 0) + line(shared_nodes, cells)
    small = ids.astype(F32) + line(inv_sqrt_mass[None], cells + 1) + line(potential[None], cells + 2)
    messages = call(
        functools.partial(pack_kernel, planes, corners),
        [((nodes + (cells + 1) // 2 * LANES + EXTRA, LANES), BF16)] * GROUP,
        (place_arg, orbital_block, cell_matrices, small),
        spaces="svvv",
        scratch=[pltpu.VMEM((cells, LANES, LANES), F32)],
    )
    messages = [messages[0]] + [in_plane(messages[k], k) for k in range(1, GROUP)]
    slabs = []
    for message in messages:
        slabs += call(
            functools.partial(build_kernel, nodes, cells, corners, shared),
            [
                ((nodes, nodes), F32), ((shared, shared), F32), ((nodes, 2 * shared), BF16), ((2 * shared, nodes), BF16),
            ] + [((nodes, LANES), F32)] * 4,
            (filter_center, filter_halfwidth, message, slabs[-7] if slabs else message),
            spaces="ssva",
            flops=1 << 28,
        )
    height = GROUP * nodes
    column = ((height, LANES), F32)
    trace = ((FILTER_DEG * shared + 2 * shared, LANES), BF16)
    odd_arg = (plane % 2).astype(jnp.int32).reshape(1)
    whole, up, mass, recip, scale, diag, start, keep, *pairs = call(
        functools.partial(first_kernel, shared),
        [
            ((GROUP, nodes + 2 * shared, nodes), BF16), ((GROUP, nodes, 2 * shared), BF16),
            column, column, column, column, ((height, LANES), BF16), ((shared, LANES), BF16), trace, trace,
        ],
        (place_arg, odd_arg, *messages, *slabs),
        spaces="ss" + "v" * (GROUP * 9),
        scratch=[
            pltpu.VMEM((GROUP, nodes, nodes), F32), pltpu.VMEM((GROUP, shared, shared), F32),
            pltpu.VMEM((height, 2 * LANES), F32), pltpu.VMEM((height, 2 * LANES), F32),
            pltpu.VMEM((2, *trace[0]), BF16),
        ],
        flops=1 << 30,
    )

    def with_neighbour(blocks):
        firsts = [z ^ 1 for z in range(planes)]
        seconds = [(z + 1 if z % 2 else z - 1) % planes for z in range(planes)]
        routes = [[(i, to[i // GROUP] * GROUP + i % GROUP) for i in everyone] for to in (firsts, seconds)]
        return [lax.ppermute(block, "dom", route) for block, route in zip(blocks, routes)]

    heard = with_neighbour(pairs)
    mine, corner, *pairs = call(
        functools.partial(second_kernel, shared),
        [((height, LANES), BF16)] + [((shared, LANES), BF16)] * 3,
        (odd_arg, whole, up, mass, recip, scale, diag, start, keep, *heard),
        spaces="s" + "v" * 10,
        scratch=[pltpu.VMEM((height, LANES), F32), pltpu.VMEM((height, LANES), F32), pltpu.VMEM((2, *trace[0]), BF16)],
        flops=1 << 30,
    )
    heard = with_neighbour(pairs)
    others = [in_plane(mine, k) for k in HELD[1:]]
    first, others[0], *heard = lax.optimization_barrier((mine, others[0], *heard))
    swapped = [[to_band(block, k) for block in (first, others[0])] for k in range(1, band_count)]
    (left,) = call(
        functools.partial(third_kernel, shared),
        [((2 * LANES, height), BF16)],
        (odd_arg, filter_center, filter_halfwidth, whole, up, mass, diag, mine, corner, *heard, *sum(swapped, [])),
        spaces="sss" + "v" * 8 + "a" * 2 * (band_count - 1),
        scratch=[pltpu.VMEM((2, shared, LANES), BF16)],
        flops=1 << 28,
    )

    gathered = [mine] + others
    rights = list(gathered)
    for k in range(1, band_count):
        rights += swapped[k - 1] + [to_band(block, k) for block in others[1:]]
    part = (2, rows, band_count * width)
    (half,) = call(product_kernel, [((2 * LANES, width), F32)], (left, *rights[:GROUP]), flops=1 << 28)
    parts = list(call(
        functools.partial(cut_kernel, planes, partner),
        [(part, F32)] + [(part, BF16)] * (planes - 1),
        (plane.astype(jnp.int32).reshape(1), left, half, *rights[GROUP:]),
        spaces="svv" + "v" * (len(rights) - GROUP),
        scratch=[pltpu.VMEM((2 * LANES, (band_count - 1) * width), F32)],
        flops=1 << 28,
    ))
    for k in [*range(2, planes), *range(1, min(planes, 2))]:
        route = [(i, partner(i // GROUP, k) * GROUP + i % GROUP) for i in everyone]
        parts[k] = lax.ppermute(parts[k], "dom", route)
    early = [*range(2, planes), 1][0]
    *gathered, parts[early] = lax.optimization_barrier((*gathered, parts[early]))
    (filtered,) = call(
        functools.partial(arrange_kernel, planes),
        [((nodes, width), BF16)],
        (place_arg, *gathered),
        spaces="s" + "v" * GROUP,
    )
    projected, intersection = call(
        functools.partial(place_kernel, planes, band_count, 1.0 / (nodes * dom_count)),
        [((rows, band_count * width), F32)] * 2,
        (place_arg, band.astype(jnp.int32).reshape(1), *parts),
        spaces="ss" + "v" * planes,
    )
    return filtered, intersection, projected


def solution(mesh):
    return jax.shard_map(
        shards,
        mesh=mesh,
        in_specs=(
            P("dom", "band"),
            P("dom", None, None),
            P(None, "dom"),
            P("dom", None),
            P("dom"),
            P("dom"),
            P(),
            P(),
        ),
        out_specs=(P("dom", "band"), P(("band", "dom"), None), P(("band", "dom"), None)),
        check_vma=False,
    )
```
